32 devices in a mesh: ctx: 8 (over z, y), head: 4 (over x, core).
Axes of the slice: x: 2, y: 2, z: 4, core: 2. Of those that a mesh axis runs over, the one named last changes fastest.
Arguments:
- queries: bfloat16 [1280, 8192], P('ctx', 'head'), may hold values from -6 to 6
- keys: bfloat16 [1280, 2048], P('ctx', 'head'), may hold values from -6 to 6
- values: bfloat16 [1280, 2048], P('ctx', 'head'), may hold values from -6 to 6
- out_grad: bfloat16 [1280, 8192], P('ctx', 'head'), may hold values from -6 to 6
- order: int32 [16], replicated, may hold values from 0 to 15, as said below
Outputs:
- attention: bfloat16 [1280, 8192], P('ctx', 'head')
- grad_queries: bfloat16 [1280, 8192], P('ctx', 'head')
- grad_keys: bfloat16 [1280, 2048], P('ctx', 'head')
- grad_values: bfloat16 [1280, 2048], P('ctx', 'head')
The draws below stay inside these ranges and needn't reach their ends.
Inputs may be any that keep to these rules, and one draw needn't show every extreme that they name: order is a permutation of the 16 spans; row blocks 2i and 2i + 1 (the rows of index i of ctx) hold spans c and 15 - c for some c, in either order.
All inputs are finite; a program needn't handle non-finite values.
Results may differ from the reference program's by a relative error of at most 0.03.
Values may be sent and summed in bfloat16 or wider, within the bound.
A program may use at most 64 MiB of HBM per device.

```python
import jax
import jax.numpy as jnp
from jax import lax

HEADS = 32
KV_HEADS = 8
HEAD_DIM = 128
BATCH = 2
SPAN = 80
NCHUNK = 16
SEQ = 1280
N_CTX = 8


def fold_order(key):
    base_key = jax.random.fold_in(key, 7)
    perm_key, flip_key = jax.random.split(base_key)
    chosen = jax.random.permutation(perm_key, N_CTX).astype(jnp.int32)
    flipped = jax.random.randint(flip_key, (N_CTX,), 0, 2, dtype=jnp.int32)
    lowhigh = jnp.stack([chosen, NCHUNK - 1 - chosen], axis=1)
    swapped = jnp.stack([lowhigh[:, 1], lowhigh[:, 0]], axis=1)
    return jnp.where(flipped[:, None] == 1, swapped, lowhigh).reshape(-1).astype(jnp.int32)


def draw_order(key, part):
    return fold_order(key)


def draw_queries(key, part):
    base_key = jax.random.fold_in(key, 21)
    drawn = jnp.clip(jax.random.normal(base_key, (SEQ, BATCH * HEADS * HEAD_DIM), jnp.float32), -6.0, 6.0)
    return drawn.astype(jnp.bfloat16)


def draw_keys(key, part):
    base_key = jax.random.fold_in(key, 22)
    drawn = jnp.clip(jax.random.normal(base_key, (SEQ, BATCH * KV_HEADS * HEAD_DIM), jnp.float32), -6.0, 6.0)
    return drawn.astype(jnp.bfloat16)


def block_scale(rng, dims, cuts, low, largest):
    def one(position, blocks):
        draws = jax.random.uniform(jax.random.fold_in(jax.random.fold_in(rng, 6), position), (blocks,), jnp.float32, low / len(cuts), largest / len(cuts))
        return jnp.repeat(jnp.exp(draws), dims[position] // blocks).reshape((-1,) + (1,) * (len(dims) - position - 1))

    loudness = one(*cuts[0])
    for cut in cuts[1:]:
        loudness = loudness * one(*cut)
    return loudness


def noise(own_key, extent, spread, most, pieces=(), held_as=jnp.bfloat16):
    result = spread * jax.random.normal(own_key, extent, jnp.float32)
    if pieces:
        result = result * block_scale(own_key, extent, pieces, -0.22, 0.18)
    return jnp.clip(result, -most, most).astype(held_as)


def setup_inputs(seed: int = 0) -> dict:
    arg_keys = jax.random.split(jax.random.key(seed), 6)
    queries = draw_queries(jax.random.fold_in(arg_keys[5], 71), 0)
    keys = draw_keys(jax.random.fold_in(arg_keys[5], 71), 0)
    values = noise(arg_keys[2], (SEQ, BATCH * KV_HEADS * HEAD_DIM), 1.0, 6.0, ((0, 8), (1, 4)))
    out_grad = noise(arg_keys[3], (SEQ, BATCH * HEADS * HEAD_DIM), 1.0, 6.0, ((0, 8), (1, 4)))
    order = draw_order(jax.random.fold_in(arg_keys[5], 71), 0)
    return {"queries": queries, "keys": keys, "values": values, "out_grad": out_grad, "order": order}


NEG = -1e30


def reference(queries, keys, values, out_grad, order):
    seq_len = queries.shape[0]
    score_scale = 1.0 / (HEAD_DIM ** 0.5)
    group_size = HEADS // KV_HEADS
    all_heads = BATCH * HEADS
    all_kv = BATCH * KV_HEADS
    row_ids = jnp.arange(seq_len, dtype=jnp.int32)
    positions = order[row_ids // SPAN] * SPAN + row_ids % SPAN
    visible = positions[None, :] <= positions[:, None]
    blocked_visible = visible.reshape(seq_len, NCHUNK, SPAN)

    def split_heads(array, head_count):
        return array.reshape(seq_len, head_count, HEAD_DIM).transpose(1, 0, 2)

    query_heads = split_heads(queries, all_heads)
    grad_heads = split_heads(out_grad, all_heads)
    key_heads = jnp.repeat(split_heads(keys, all_kv), group_size, axis=0)
    value_heads = jnp.repeat(split_heads(values, all_kv), group_size, axis=0)

    def one_head(inputs):
        query_h, key_h, value_h, grad_h = inputs
        scores = jnp.dot(query_h, key_h.T, preferred_element_type=jnp.float32) * score_scale
        scores = jnp.where(visible, scores, NEG)
        blocked = scores.reshape(seq_len, NCHUNK, SPAN)
        block_max = jnp.max(blocked, axis=2)
        block_weights = jnp.where(blocked_visible, jnp.exp(blocked - block_max[:, :, None]), 0.0)
        block_total = jnp.sum(block_weights, axis=2)
        weights_low = lax.optimization_barrier(block_weights.astype(jnp.bfloat16)).astype(jnp.float32)
        row_max = jnp.max(block_max, axis=1)
        block_factor = jnp.exp(block_max - row_max[:, None])
        row_total = jnp.sum(block_factor * block_total, axis=1)
        scaled_weights = (block_factor[:, :, None] * weights_low).reshape(seq_len, seq_len)
        attention = jnp.dot(scaled_weights, value_h.astype(jnp.float32), precision=lax.Precision.HIGHEST)
        attention = (attention / row_total[:, None]).astype(jnp.bfloat16)
        log_total = row_max + jnp.log(row_total)
        row_dot = jnp.sum(grad_h.astype(jnp.float32) * attention.astype(jnp.float32), axis=1)
        probs = jnp.where(visible, jnp.exp(scores - log_total[:, None]), 0.0)
        probs_low = probs.astype(jnp.bfloat16)
        grad_value = jnp.dot(probs_low.T, grad_h, preferred_element_type=jnp.float32)
        grad_probs = jnp.dot(grad_h, value_h.T, preferred_element_type=jnp.float32)
        grad_scores = (probs * (grad_probs - row_dot[:, None])).astype(jnp.bfloat16)
        grad_query = jnp.dot(grad_scores, key_h, preferred_element_type=jnp.float32)
        grad_key = jnp.dot(grad_scores.T, query_h, preferred_element_type=jnp.float32)
        return attention, grad_query, grad_key, grad_value

    attention, grad_query, grad_key, grad_value = lax.map(one_head, (query_heads, key_heads, value_heads, grad_heads))

    def join_heads(array):
        return array.transpose(1, 0, 2).reshape(seq_len, -1)

    grad_key = jnp.sum(grad_key.reshape(all_kv, group_size, seq_len, HEAD_DIM), axis=1)
    grad_value = jnp.sum(grad_value.reshape(all_kv, group_size, seq_len, HEAD_DIM), axis=1)
    grad_queries = join_heads((score_scale * grad_query).astype(jnp.bfloat16))
    grad_keys = join_heads((score_scale * grad_key).astype(jnp.bfloat16))
    grad_values = join_heads(grad_value.astype(jnp.bfloat16))
    return (join_heads(attention), grad_queries, grad_keys, grad_values)
```

```python
import functools
import math

import jax
import jax.numpy as jnp
from jax import lax
from jax.experimental import pallas as pl
from jax.experimental.pallas import tpu as pltpu
from jax.sharding import PartitionSpec as P

HEADS = 32
KV_HEADS = 8
HEAD_DIM = 128
GROUP = HEADS // KV_HEADS
NEG = -1e30
MESH = pl.DeviceIdType.MESH

UP, DOWN = 0, 1


def line_lengths(n_ctx):
    n0 = 4 if n_ctx % 4 == 0 else 1
    return n0, n_ctx // n0


def dot_nt(a, b):
    return lax.dot_general(a, b, (((1,), (1,)), ((), ())), preferred_element_type=jnp.float32)


def dot_tn(a, b):
    return lax.dot_general(a, b, (((0,), (0,)), ((), ())), preferred_element_type=jnp.float32)


def dot_nn(a, b):
    return lax.dot_general(a, b, (((1,), (0,)), ((), ())), preferred_element_type=jnp.float32)


def kernel(
    n_ctx, kv_heads, rows, chunk, kinds,
    q_ref, k_ref, v_ref, g_ref, order_ref,
    att_ref, dq_ref, dk_ref, dv_ref,
    kv, bias, probs, qs, gs, att_t, dq_t, acc,
    send_s, recv_s, send_f, recv_f,
    ag_send, ag_recv, s_send, s_recv, f_send, f_recv,
):
    n0, n1 = line_lengths(n_ctx)
    me = lax.axis_index("ctx")
    i0, i1 = me // n1, me % n1
    span = rows // 2
    keys_all = n_ctx * rows
    q_rows = GROUP * rows
    scale = 1.0 / math.sqrt(HEAD_DIM)
    to_exp2 = scale * math.log2(math.e)

    class Kind:
        def __init__(self, index):
            self.index = index
            first_is_0 = kinds[index] == 0
            self.nf, self.ns = (n0, n1) if first_is_0 else (n1, n0)
            self.f, self.s = (i0, i1) if first_is_0 else (i1, i0)
            self.first_is_0 = first_is_0

        def device(self, f, s):
            return f * n1 + s if self.first_is_0 else s * n1 + f

        def slot(self, f, s):
            return s * self.nf + f

        def neighbour(self, line, direction):
            step = 1 if direction == UP else -1
            if line == 0:
                return self.device(self.f + step, self.s)
            return self.device(self.f, self.s + step)

        def has(self, line, direction):
            x, n = (self.f, self.nf) if line == 0 else (self.s, self.ns)
            return x + 1 < n if direction == UP else x > 0

    kind_list = [Kind(i) for i in range(len(kinds))]

    def kind_of(h):
        return kind_list[h % len(kinds)]

    def block(slot):
        return pl.ds(pl.multiple_of(slot * rows, rows), rows)

    barrier = pltpu.get_barrier_semaphore()
    base = kind_list[0]
    for line in (0, 1):
        for direction in (UP, DOWN):
            @pl.when(base.has(line, direction))
            def _(line=line, direction=direction):
                pl.semaphore_signal(
                    barrier, inc=1, device_id={"ctx": base.neighbour(line, direction)},
                    device_id_type=MESH,
                )
    peers = sum(
        base.has(line, direction).astype(jnp.int32) for line in (0, 1) for direction in (UP, DOWN)
    )
    pl.semaphore_wait(barrier, peers)

    def ag_copy(h, slot, line, direction):
        kind = kind_of(h)
        return pltpu.make_async_remote_copy(
            src_ref=kv.at[h, block(slot)],
            dst_ref=kv.at[h, block(slot)],
            send_sem=ag_send.at[h, slot, 2 * line + direction],
            recv_sem=ag_recv.at[h, slot],
            device_id={"ctx": kind.neighbour(line, direction)},
            device_id_type=MESH,
        )

    def ag_stage(h, stage, op):
        kind = kind_of(h)
        nf, ns, f, s = kind.nf, kind.ns, kind.f, kind.s

        def push(slot, line, direction):
            @pl.when(kind.has(line, direction))
            def _():
                copy = ag_copy(h, slot, line, direction)
                if op == "go":
                    copy.start()
                else:
                    copy.wait_send()

        def arrived(slot):
            if op == "go":
                ag_copy(h, slot, 0, UP).wait_recv()

        if stage == 0:
            own = kind.slot(f, s)
            if op == "go":
                columns = pl.ds(h * HEAD_DIM, HEAD_DIM)
                kv[h, block(own), 0:HEAD_DIM] = k_ref[:, columns]
                kv[h, block(own), HEAD_DIM:] = v_ref[:, columns]
            for line in (0, 1):
                push(own, line, UP)
                push(own, line, DOWN)
        elif stage < nf:
            for origin, direction in ((f - stage, UP), (f + stage, DOWN)):
                @pl.when(jnp.logical_and(origin >= 0, origin < nf))
                def _(origin=origin, direction=direction):
                    slot = kind.slot(origin, s)
                    arrived(slot)
                    push(slot, 0, direction)
                    push(slot, 1, UP)
                    push(slot, 1, DOWN)
        else:
            d = stage - nf + 1
            for origin, direction in ((s - d, UP), (s + d, DOWN)):
                @pl.when(jnp.logical_and(origin >= 0, origin < ns))
                def _(origin=origin, direction=direction):
                    for from_f in range(nf):
                        slot = kind.slot(from_f, origin)
                        arrived(slot)
                        push(slot, 1, direction)

    def ag_stages(h):
        return kind_of(h).nf + kind_of(h).ns - 1

    def line_copy(h, line, x, direction):
        kind = kind_of(h)
        if line == 1:
            size = kind.nf * rows
            where = pl.ds(pl.multiple_of(x * size, size), size)
            src, dst, sends, recvs = send_s, recv_s, s_send, s_recv
        else:
            where = block(x)
            src, dst, sends, recvs = send_f, recv_f, f_send, f_recv
        return pltpu.make_async_remote_copy(
            src_ref=src.at[h, where],
            dst_ref=dst.at[h, direction, where],
            send_sem=sends.at[h, x],
            recv_sem=recvs.at[h, direction, x],
            device_id={"ctx": kind.neighbour(line, direction)},
            device_id_type=MESH,
        )

    def acc_rows(h, line, x):
        kind = kind_of(h)
        if line == 1:
            size = kind.nf * rows
            return pl.ds(pl.multiple_of(x * size, size), size)
        return block(kind.slot(x, kind.s))

    def line_rows(h, line, x):
        kind = kind_of(h)
        size = kind.nf * rows if line == 1 else rows
        return pl.ds(pl.multiple_of(x * size, size), size)

    def chain_stage(h, line, stage, op):
        kind = kind_of(h)
        at, n = (kind.f, kind.nf) if line == 0 else (kind.s, kind.ns)
        src, dst = (send_f, recv_f) if line == 0 else (send_s, recv_s)

        def pass_on(x, direction):
            copy = line_copy(h, line, x, direction)
            if op == "sent":
                copy.wait_send()
                return
            total = acc[h, acc_rows(h, line, x)]
            if stage > 0:
                copy.wait_recv()
                total = total + dst[h, direction, line_rows(h, line, x)].astype(jnp.float32)
            src[h, line_rows(h, line, x)] = total.astype(jnp.bfloat16)
            copy.start()

        @pl.when(at == stage)
        def _():
            for x in range(n - 1, stage, -1):
                pass_on(x, UP)

        @pl.when(at == n - 1 - stage)
        def _():
            for x in range(0, n - 1 - stage):
                pass_on(x, DOWN)

    def chain_end(h, line):
        kind = kind_of(h)
        at, n = (kind.f, kind.nf) if line == 0 else (kind.s, kind.ns)
        dst = recv_f if line == 0 else recv_s
        for direction, there in ((UP, at > 0), (DOWN, at < n - 1)):
            @pl.when(there)
            def _(direction=direction):
                line_copy(h, line, at, direction).wait_recv()
                where = acc_rows(h, line, at)
                acc[h, where] = acc[h, where] + dst[
                    h, direction, line_rows(h, line, at)
                ].astype(jnp.float32)

    def write_kv_grads(h):
        kind = kind_of(h)
        where = block(kind.slot(kind.f, kind.s))
        columns = pl.ds(h * HEAD_DIM, HEAD_DIM)
        dk_ref[:, columns] = (acc[h, where, 0:HEAD_DIM] * scale).astype(jnp.bfloat16)
        dv_ref[:, columns] = acc[h, where, HEAD_DIM:].astype(jnp.bfloat16)

    def rs_tasks(h):
        kind = kind_of(h)
        tasks = []
        for stage in range(1, kind.ns - 1):
            tasks.append(functools.partial(chain_stage, h, 1, stage, "go"))

        def turn():
            chain_end(h, 1)
            chain_stage(h, 0, 0, "go")

        tasks.append(turn)
        for stage in range(1, kind.nf - 1):
            tasks.append(functools.partial(chain_stage, h, 0, stage, "go"))

        def finish():
            chain_end(h, 0)
            write_kv_grads(h)

        tasks.append(finish)
        return tasks

    def make_bias(kind):
        lane = lax.broadcasted_iota(jnp.int32, (1, q_rows), 1) % rows
        low, high = order_ref[2 * me], order_ref[2 * me + 1]
        q_pos = jnp.where(lane < span, low * span + lane, high * span + lane - span)
        row = lax.broadcasted_iota(jnp.int32, (span, q_rows), 0)

        @pl.loop(0, n_ctx)
        def _(slot):
            source = kind.device(slot % kind.nf, slot // kind.nf)
            for half in range(2):
                k_pos = row + order_ref[2 * source + half] * span
                where = pl.ds(pl.multiple_of(slot * rows + half * span, span), span)
                bias[kind.index, where] = jnp.where(k_pos <= q_pos, 0.0, NEG)

    def load_queries(h):
        for g in range(GROUP):
            columns = pl.ds((h * GROUP + g) * HEAD_DIM, HEAD_DIM)
            qs[pl.ds(g * rows, rows)] = q_ref[:, columns]
            gs[pl.ds(g * rows, rows)] = g_ref[:, columns]

    def rows_of(i):
        return pl.ds(pl.multiple_of(i * chunk, chunk), chunk)

    def fold(x, op):
        return op(x.reshape(chunk // 8, 8, q_rows), axis=0)

    def scores_pass(h):
        kind = kind_of(h)

        def body(i, top):
            where = rows_of(i)
            s = dot_nt(kv[h, where, 0:HEAD_DIM], qs[...]) + bias[kind.index, where]
            probs[where] = s
            return jnp.maximum(top, fold(s, jnp.max))

        top = lax.fori_loop(
            0, keys_all // chunk, body, jnp.full((8, q_rows), NEG, jnp.float32)
        )
        return jnp.max(top, axis=0, keepdims=True) * to_exp2

    def weights_pass(h, top):
        att_t[...] = jnp.zeros_like(att_t)

        def body(i, total):
            where = rows_of(i)
            e = jnp.exp2(probs[where] * to_exp2 - top)
            probs[where] = e
            att_t[...] += dot_tn(kv[h, where, HEAD_DIM:], e.astype(jnp.bfloat16))
            return total + fold(e, jnp.sum)

        total = lax.fori_loop(
            0, keys_all // chunk, body, jnp.zeros((8, q_rows), jnp.float32)
        )
        inverse = 1.0 / jnp.sum(total, axis=0, keepdims=True)
        attention = (att_t[...] * inverse).T.astype(jnp.bfloat16)
        for g in range(GROUP):
            columns = pl.ds((h * GROUP + g) * HEAD_DIM, HEAD_DIM)
            att_ref[:, columns] = attention[g * rows:(g + 1) * rows]
        product = gs[...].astype(jnp.float32) * attention.astype(jnp.float32)
        row_dot = jnp.sum(product.T, axis=0, keepdims=True)
        return inverse, row_dot

    def backward_group(h, s, inverse, row_dot):
        kind = kind_of(h)
        per_group = kind.nf * rows // chunk

        @pl.loop(0, per_group)
        def _(j):
            where = rows_of(s * per_group + j)
            k, v = kv[h, where, 0:HEAD_DIM], kv[h, where, HEAD_DIM:]
            p = probs[where] * inverse
            ds = (p * (dot_nt(v, gs[...]) - row_dot)).astype(jnp.bfloat16)
            acc[h, where, 0:HEAD_DIM] = dot_nn(ds, qs[...])
            acc[h, where, HEAD_DIM:] = dot_nn(p.astype(jnp.bfloat16), gs[...])
            dq_t[...] += dot_tn(k, ds)

    def write_dq(h):
        dq = (dq_t[...] * scale).T.astype(jnp.bfloat16)
        for g in range(GROUP):
            columns = pl.ds((h * GROUP + g) * HEAD_DIM, HEAD_DIM)
            dq_ref[:, columns] = dq[g * rows:(g + 1) * rows]

    lag = 2
    ticks = []
    last_tick = lag * (kv_heads - 1) + max(ag_stages(h) for h in range(kv_heads))
    for t in range(last_tick):
        ticks.append([
            (h, t - lag * h) for h in range(kv_heads) if 0 <= t - lag * h < ag_stages(h)
        ])
    done = 0

    def run_ticks(until):
        nonlocal done
        while done < min(until, len(ticks)):
            for h, stage in ticks[done]:
                ag_stage(h, stage, "go")
            done += 1

    pending = []

    def run_pending(count):
        for _ in range(min(count, len(pending))):
            pending.pop(0)()

    run_ticks(1)
    for kind in kind_list:
        make_bias(kind)
    load_queries(0)
    for h in range(kv_heads):
        kind = kind_of(h)
        run_ticks(lag * h + ag_stages(h))
        if h:
            load_queries(h)
        top = scores_pass(h)
        run_ticks(lag * h + ag_stages(h) + 1)
        run_pending(1)
        inverse, row_dot = weights_pass(h, top)
        run_ticks(lag * h + ag_stages(h) + 2)
        run_pending(1)
        dq_t[...] = jnp.zeros_like(dq_t)

        def away(j, _):
            backward_group(h, lax.rem(kind.s + j, kind.ns), inverse, row_dot)
            return 0

        lax.fori_loop(1, kind.ns, away, 0)
        run_pending(1)
        chain_stage(h, 1, 0, "go")
        backward_group(h, kind.s, inverse, row_dot)
        run_pending(len(pending))
        write_dq(h)
        pending.extend(rs_tasks(h))
    run_pending(len(pending))

    for h in range(kv_heads):
        for stage in range(ag_stages(h)):
            ag_stage(h, stage, "sent")
        for line in (1, 0):
            kind = kind_of(h)
            for stage in range((kind.ns if line else kind.nf) - 1):
                chain_stage(h, line, stage, "sent")


def on_device(n_ctx, queries, keys, values, out_grad, order):
    rows = queries.shape[0]
    kv_heads = keys.shape[1] // HEAD_DIM
    q_rows = GROUP * rows
    keys_all = n_ctx * rows
    n0, n1 = line_lengths(n_ctx)
    kinds = (0, 1) if kv_heads > 1 else (0,)
    wide = 2 * HEAD_DIM
    longest = max(n0, n1)
    chunk = 2 * rows
    vmem = pl.BlockSpec(memory_space=pltpu.VMEM)
    return pl.pallas_call(
        functools.partial(kernel, n_ctx, kv_heads, rows, chunk, kinds),
        out_shape=[
            jax.ShapeDtypeStruct(x.shape, jnp.bfloat16) for x in (queries, queries, keys, values)
        ],
        in_specs=[vmem] * 4 + [pl.BlockSpec(memory_space=pltpu.SMEM)],
        out_specs=[vmem] * 4,
        scratch_shapes=[
            pltpu.VMEM((kv_heads, keys_all, wide), jnp.bfloat16),
            pltpu.VMEM((len(kinds), keys_all, q_rows), jnp.float32),
            pltpu.VMEM((keys_all, q_rows), jnp.float32),
            pltpu.VMEM((q_rows, HEAD_DIM), jnp.bfloat16),
            pltpu.VMEM((q_rows, HEAD_DIM), jnp.bfloat16),
            pltpu.VMEM((HEAD_DIM, q_rows), jnp.float32),
            pltpu.VMEM((HEAD_DIM, q_rows), jnp.float32),
            pltpu.VMEM((kv_heads, keys_all, wide), jnp.float32),
            pltpu.VMEM((kv_heads, keys_all, wide), jnp.bfloat16),
            pltpu.VMEM((kv_heads, 2, keys_all, wide), jnp.bfloat16),
            pltpu.VMEM((kv_heads, longest * rows, wide), jnp.bfloat16),
            pltpu.VMEM((kv_heads, 2, longest * rows, wide), jnp.bfloat16),
            pltpu.SemaphoreType.DMA((kv_heads, n_ctx, 4)),
            pltpu.SemaphoreType.DMA((kv_heads, n_ctx)),
            pltpu.SemaphoreType.DMA((kv_heads, longest)),
            pltpu.SemaphoreType.DMA((kv_heads, 2, longest)),
            pltpu.SemaphoreType.DMA((kv_heads, longest)),
            pltpu.SemaphoreType.DMA((kv_heads, 2, longest)),
        ],
        compiler_params=pltpu.CompilerParams(
            collective_id=0, has_side_effects=True, vmem_limit_bytes=60 * 1024 * 1024
        ),
        name="attention_fwd_bwd",
    )(queries, keys, values, out_grad, order)


def solution(mesh):
    return jax.shard_map(
        functools.partial(on_device, mesh.shape["ctx"]),
        mesh=mesh,
        in_specs=(P("ctx", "head"), P("ctx", "head"), P("ctx", "head"), P("ctx", "head"), P()),
        out_specs=(P("ctx", "head"), P("ctx", "head"), P("ctx", "head"), P("ctx", "head")),
        check_vma=False,
    )
```

```python
import functools
import math

import jax
import jax.numpy as jnp
from jax import lax
from jax.experimental import pallas as pl
from jax.experimental.pallas import tpu as pltpu
from jax.sharding import PartitionSpec as P

HEADS = 32
KV_HEADS = 8
HEAD_DIM = 128
GROUP = HEADS // KV_HEADS
NEG = -1e30
MESH = pl.DeviceIdType.MESH

UP, DOWN = 0, 1


def line_lengths(n_ctx):
    n0 = 4 if n_ctx % 4 == 0 else 1
    return n0, n_ctx // n0


def dot_nt(a, b):
    return lax.dot_general(a, b, (((1,), (1,)), ((), ())), preferred_element_type=jnp.float32)


def dot_tn(a, b):
    return lax.dot_general(a, b, (((0,), (0,)), ((), ())), preferred_element_type=jnp.float32)


def dot_nn(a, b):
    return lax.dot_general(a, b, (((1,), (0,)), ((), ())), preferred_element_type=jnp.float32)


def kernel(
    n_ctx, kv_heads, rows, chunk, kinds,
    q_ref, k_ref, v_ref, g_ref, order_ref,
    att_ref, dq_ref, dk_ref, dv_ref,
    kv, bias, probs, qs, gs, att_t, dq_t, acc,
    send_s, recv_s, send_f, recv_f,
    ag_send, ag_recv, s_send, s_recv, f_send, f_recv,
):
    n0, n1 = line_lengths(n_ctx)
    me = lax.axis_index("ctx")
    i0, i1 = me // n1, me % n1
    span = rows // 2
    keys_all = n_ctx * rows
    q_rows = GROUP * rows
    scale = 1.0 / math.sqrt(HEAD_DIM)
    to_exp2 = scale * math.log2(math.e)

    class Kind:
        def __init__(self, index):
            self.index = index
            first_is_0 = kinds[index] == 0
            self.nf, self.ns = (n0, n1) if first_is_0 else (n1, n0)
            self.f, self.s = (i0, i1) if first_is_0 else (i1, i0)
            self.first_is_0 = first_is_0

        def device(self, f, s):
            return f * n1 + s if self.first_is_0 else s * n1 + f

        def slot(self, f, s):
            return s * self.nf + f

        def neighbour(self, line, direction):
            step = 1 if direction == UP else -1
            if line == 0:
                return self.device(self.f + step, self.s)
            return self.device(self.f, self.s + step)

        def has(self, line, direction):
            x, n = (self.f, self.nf) if line == 0 else (self.s, self.ns)
            return x + 1 < n if direction == UP else x > 0

    kind_list = [Kind(i) for i in range(len(kinds))]

    def kind_of(h):
        return kind_list[1 if h % 4 == 1 else 0]

    def block(slot):
        return pl.ds(pl.multiple_of(slot * rows, rows), rows)

    barrier = pltpu.get_barrier_semaphore()
    base = kind_list[0]
    for line in (0, 1):
        for direction in (UP, DOWN):
            @pl.when(base.has(line, direction))
            def _(line=line, direction=direction):
                pl.semaphore_signal(
                    barrier, inc=1, device_id={"ctx": base.neighbour(line, direction)},
                    device_id_type=MESH,
                )
    peers = sum(
        base.has(line, direction).astype(jnp.int32) for line in (0, 1) for direction in (UP, DOWN)
    )
    pl.semaphore_wait(barrier, peers)

    def ag_copy(h, slot, line, direction):
        kind = kind_of(h)
        return pltpu.make_async_remote_copy(
            src_ref=kv.at[h, block(slot)],
            dst_ref=kv.at[h, block(slot)],
            send_sem=ag_send.at[h, slot, 2 * line + direction],
            recv_sem=ag_recv.at[h, slot],
            device_id={"ctx": kind.neighbour(line, direction)},
            device_id_type=MESH,
        )

    def ag_stage(h, stage, op):
        kind = kind_of(h)
        nf, ns, f, s = kind.nf, kind.ns, kind.f, kind.s

        def push(slot, line, direction):
            @pl.when(kind.has(line, direction))
            def _():
                copy = ag_copy(h, slot, line, direction)
                if op == "go":
                    copy.start()
                else:
                    copy.wait_send()

        def arrived(slot):
            if op == "go":
                ag_copy(h, slot, 0, UP).wait_recv()

        if stage == 0:
            own = kind.slot(f, s)
            if op == "go":
                columns = pl.ds(h * HEAD_DIM, HEAD_DIM)
                kv[h, block(own), 0:HEAD_DIM] = k_ref[:, columns]
                kv[h, block(own), HEAD_DIM:] = v_ref[:, columns]
            for line in (0, 1):
                push(own, line, UP)
                push(own, line, DOWN)
        elif stage < nf:
            for origin, direction in ((f - stage, UP), (f + stage, DOWN)):
                @pl.when(jnp.logical_and(origin >= 0, origin < nf))
                def _(origin=origin, direction=direction):
                    slot = kind.slot(origin, s)
                    arrived(slot)
                    push(slot, 0, direction)
                    push(slot, 1, UP)
                    push(slot, 1, DOWN)
        else:
            d = stage - nf + 1
            for origin, direction in ((s - d, UP), (s + d, DOWN)):
                @pl.when(jnp.logical_and(origin >= 0, origin < ns))
                def _(origin=origin, direction=direction):
                    for from_f in range(nf):
                        slot = kind.slot(from_f, origin)
                        arrived(slot)
                        push(slot, 1, direction)

    def ag_stages(h):
        return kind_of(h).nf + kind_of(h).ns - 1

    def s_copy(h, slot, direction):
        kind = kind_of(h)
        return pltpu.make_async_remote_copy(
            src_ref=send_s.at[h, block(slot)],
            dst_ref=recv_s.at[h, direction, block(slot)],
            send_sem=s_send.at[h, slot],
            recv_sem=s_recv.at[h, direction, slot],
            device_id={"ctx": kind.device(kind.f, kind.s + 1 - 2 * direction)},
            device_id_type=MESH,
        )

    def f_copy(h, x, direction):
        kind = kind_of(h)
        return pltpu.make_async_remote_copy(
            src_ref=send_f.at[h, block(x)],
            dst_ref=recv_f.at[h, direction, block(x)],
            send_sem=f_send.at[h, x],
            recv_sem=f_recv.at[h, direction, x],
            device_id={"ctx": kind.neighbour(0, direction)},
            device_id_type=MESH,
        )

    def s_pass_on(h, slot, direction, first):
        total = acc[h, block(slot)]
        copy = s_copy(h, slot, direction)
        if not first:
            copy.wait_recv()
            total = total + recv_s[h, direction, block(slot)].astype(jnp.float32)
        send_s[h, block(slot)] = total.astype(jnp.bfloat16)
        copy.start()

    def s_stage(h, stage):
        kind = kind_of(h)
        n = kind.ns

        @pl.when(kind.s == stage)
        def _():
            for x in range(n - 1, stage, -1):
                for f in range(kind.nf):
                    s_pass_on(h, kind.slot(f, x), UP, False)

        @pl.when(kind.s == n - 1 - stage)
        def _():
            for x in range(0, n - 1 - stage):
                for f in range(kind.nf):
                    s_pass_on(h, kind.slot(f, x), DOWN, False)

    def take_s(h, slot):
        kind = kind_of(h)
        for direction, there in ((UP, kind.s > 0), (DOWN, kind.s < kind.ns - 1)):
            @pl.when(there)
            def _(direction=direction):
                s_copy(h, slot, direction).wait_recv()
                where = block(slot)
                acc[h, where] = acc[h, where] + recv_s[h, direction, where].astype(jnp.float32)

    def f_stage(h, stage):
        kind = kind_of(h)
        n = kind.nf

        def pass_on(x, direction):
            slot = kind.slot(x, kind.s)
            take_s(h, slot)
            total = acc[h, block(slot)]
            copy = f_copy(h, x, direction)
            if stage > 0:
                copy.wait_recv()
                total = total + recv_f[h, direction, block(x)].astype(jnp.float32)
            send_f[h, block(x)] = total.astype(jnp.bfloat16)
            copy.start()

        @pl.when(kind.f == stage)
        def _():
            for x in range(n - 1, stage, -1):
                pass_on(x, UP)

        @pl.when(kind.f == n - 1 - stage)
        def _():
            for x in range(0, n - 1 - stage):
                pass_on(x, DOWN)

    def finish(h):
        kind = kind_of(h)
        own = kind.slot(kind.f, kind.s)
        take_s(h, own)
        where = block(own)
        for direction, there in ((UP, kind.f > 0), (DOWN, kind.f < kind.nf - 1)):
            @pl.when(there)
            def _(direction=direction):
                f_copy(h, kind.f, direction).wait_recv()
                acc[h, where] = acc[h, where] + recv_f[
                    h, direction, block(kind.f)
                ].astype(jnp.float32)
        columns = pl.ds(h * HEAD_DIM, HEAD_DIM)
        dk_ref[:, columns] = (acc[h, where, 0:HEAD_DIM] * scale).astype(jnp.bfloat16)
        dv_ref[:, columns] = acc[h, where, HEAD_DIM:].astype(jnp.bfloat16)

    def rs_tasks(h):
        kind = kind_of(h)
        tasks = [functools.partial(s_stage, h, stage) for stage in range(1, kind.ns - 1)]
        tasks += [functools.partial(f_stage, h, stage) for stage in range(kind.nf - 1)]
        return tasks + [functools.partial(finish, h)]

    def make_bias(kind):
        lane = lax.broadcasted_iota(jnp.int32, (1, q_rows), 1) % rows
        low, high = order_ref[2 * me], order_ref[2 * me + 1]
        q_pos = jnp.where(lane < span, low * span + lane, high * span + lane - span)
        row = lax.broadcasted_iota(jnp.int32, (span, q_rows), 0)

        @pl.loop(0, n_ctx)
        def _(slot):
            source = kind.device(slot % kind.nf, slot // kind.nf)
            for half in range(2):
                k_pos = row + order_ref[2 * source + half] * span
                where = pl.ds(pl.multiple_of(slot * rows + half * span, span), span)
                bias[kind.index, where] = jnp.where(k_pos <= q_pos, 0.0, NEG)

    def load_queries(h):
        for g in range(GROUP):
            columns = pl.ds((h * GROUP + g) * HEAD_DIM, HEAD_DIM)
            qs[pl.ds(g * rows, rows)] = q_ref[:, columns]
            gs[pl.ds(g * rows, rows)] = g_ref[:, columns]

    def rows_of(i, size):
        return pl.ds(pl.multiple_of(i * size, size), size)

    tall = 2 * chunk

    def fold(x, op):
        return op(x.reshape(tall // 8, 8, q_rows), axis=0)

    def scores_pass(h):
        kind = kind_of(h)

        def body(i, top):
            where = rows_of(i, tall)
            s = dot_nt(kv[h, where, 0:HEAD_DIM], qs[...]) + bias[kind.index, where]
            probs[where] = s
            return jnp.maximum(top, fold(s, jnp.max))

        top = lax.fori_loop(
            0, keys_all // tall, body, jnp.full((8, q_rows), NEG, jnp.float32)
        )
        return jnp.max(top, axis=0, keepdims=True) * to_exp2

    def weights_pass(h, top):
        att_t[...] = jnp.zeros_like(att_t)

        def body(i, total):
            where = rows_of(i, tall)
            e = jnp.exp2(probs[where] * to_exp2 - top)
            probs[where] = e
            att_t[...] += dot_tn(kv[h, where, HEAD_DIM:], e.astype(jnp.bfloat16))
            return total + fold(e, jnp.sum)

        total = lax.fori_loop(
            0, keys_all // tall, body, jnp.zeros((8, q_rows), jnp.float32)
        )
        inverse = 1.0 / jnp.sum(total, axis=0, keepdims=True)
        attention = (att_t[...] * inverse).T.astype(jnp.bfloat16)
        for g in range(GROUP):
            columns = pl.ds((h * GROUP + g) * HEAD_DIM, HEAD_DIM)
            att_ref[:, columns] = attention[g * rows:(g + 1) * rows]
        product = gs[...].astype(jnp.float32) * attention.astype(jnp.float32)
        row_dot = jnp.sum(product.T, axis=0, keepdims=True)
        return inverse, row_dot

    def backward_group(h, s, inverse, row_dot, send):
        kind = kind_of(h)
        per_group = kind.nf * rows // chunk
        direction = jnp.where(s > kind.s, UP, DOWN)
        first = jnp.logical_or(
            jnp.logical_and(s > kind.s, kind.s == 0),
            jnp.logical_and(s < kind.s, kind.s == kind.ns - 1),
        )
        backwards = kind.f < kind.nf // 2

        def body(j, _):
            j = jnp.where(backwards, per_group - 1 - j, j)
            where = rows_of(s * per_group + j, chunk)
            k, v = kv[h, where, 0:HEAD_DIM], kv[h, where, HEAD_DIM:]
            p = probs[where] * inverse
            ds = (p * (dot_nt(v, gs[...]) - row_dot)).astype(jnp.bfloat16)
            acc[h, where, 0:HEAD_DIM] = dot_nn(ds, qs[...])
            acc[h, where, HEAD_DIM:] = dot_nn(p.astype(jnp.bfloat16), gs[...])
            dq_t[...] += dot_tn(k, ds)
            if send:
                @pl.when(first)
                def _():
                    per_chunk = chunk // rows
                    for b in range(per_chunk):
                        b = jnp.where(backwards, per_chunk - 1 - b, b)
                        s_pass_on(h, (s * per_group + j) * per_chunk + b, direction, True)
            return 0

        lax.fori_loop(0, per_group, body, 0)

    def write_dq(h):
        dq = (dq_t[...] * scale).T.astype(jnp.bfloat16)
        for g in range(GROUP):
            columns = pl.ds((h * GROUP + g) * HEAD_DIM, HEAD_DIM)
            dq_ref[:, columns] = dq[g * rows:(g + 1) * rows]

    lag = 2
    ticks = []
    last_tick = lag * (kv_heads - 1) + max(ag_stages(h) for h in range(kv_heads))
    for t in range(last_tick):
        ticks.append([
            (h, t - lag * h) for h in range(kv_heads) if 0 <= t - lag * h < ag_stages(h)
        ])
    done = 0

    def run_ticks(until):
        nonlocal done
        while done < min(until, len(ticks)):
            for h, stage in ticks[done]:
                ag_stage(h, stage, "go")
            done += 1

    chains = []

    def advance():
        for chain in list(chains):
            chain.pop(0)()
            if not chain:
                chains.remove(chain)

    run_ticks(1)
    for kind in kind_list:
        make_bias(kind)
    load_queries(0)
    for h in range(kv_heads):
        kind = kind_of(h)
        run_ticks(lag * h + ag_stages(h))
        if h:
            load_queries(h)
        top = scores_pass(h)
        run_ticks(lag * h + ag_stages(h) + 1)
        inverse, row_dot = weights_pass(h, top)
        run_ticks(lag * h + ag_stages(h) + 2)
        advance()
        dq_t[...] = jnp.zeros_like(dq_t)

        def away(j, _):
            backward_group(h, lax.rem(kind.s + j, kind.ns), inverse, row_dot, True)
            return 0

        lax.fori_loop(1, kind.ns, away, 0)
        backward_group(h, kind.s, inverse, row_dot, False)
        advance()
        chains.append(rs_tasks(h))
        if h == kv_heads - 1:
            advance()
        write_dq(h)
    while chains:
        advance()

    for h in range(kv_heads):
        kind = kind_of(h)
        for stage in range(ag_stages(h)):
            ag_stage(h, stage, "sent")

        def sent(j, _):
            group = lax.rem(kind.s + j, kind.ns)
            for f in range(kind.nf):
                s_copy(h, kind.slot(f, group), UP).wait_send()
            return 0

        lax.fori_loop(1, kind.ns, sent, 0)
        for j in range(1, kind.nf):
            f_copy(h, lax.rem(kind.f + j, kind.nf), UP).wait_send()


def copy_kernel(*refs):
    sems = refs[-1]
    count = (len(refs) - 1) // 2
    copies = [
        pltpu.make_async_copy(refs[i], refs[count + i], sems.at[i]) for i in range(count)
    ]
    for copy in copies:
        copy.start()
    for copy in copies:
        copy.wait()


def hand_out(results):
    anywhere = pl.BlockSpec(memory_space=pl.ANY)
    return pl.pallas_call(
        copy_kernel,
        out_shape=[jax.ShapeDtypeStruct(x.shape, x.dtype) for x in results],
        in_specs=[anywhere] * len(results),
        out_specs=[anywhere] * len(results),
        scratch_shapes=[pltpu.SemaphoreType.DMA((len(results),))],
        name="hand_out",
    )(*results)


def on_device(n_ctx, queries, keys, values, out_grad, order):
    rows = queries.shape[0]
    kv_heads = keys.shape[1] // HEAD_DIM
    q_rows = GROUP * rows
    keys_all = n_ctx * rows
    n0, n1 = line_lengths(n_ctx)
    kinds = (0, 1) if kv_heads > 1 else (0,)
    wide = 2 * HEAD_DIM
    longest = max(n0, n1)
    chunk = 2 * rows
    vmem = pl.BlockSpec(memory_space=pltpu.VMEM)
    results = pl.pallas_call(
        functools.partial(kernel, n_ctx, kv_heads, rows, chunk, kinds),
        out_shape=[
            jax.ShapeDtypeStruct(x.shape, jnp.bfloat16) for x in (queries, queries, keys, values)
        ],
        in_specs=[vmem] * 4 + [pl.BlockSpec(memory_space=pltpu.SMEM)],
        out_specs=[vmem] * 4,
        scratch_shapes=[
            pltpu.VMEM((kv_heads, keys_all, wide), jnp.bfloat16),
            pltpu.VMEM((len(kinds), keys_all, q_rows), jnp.float32),
            pltpu.VMEM((keys_all, q_rows), jnp.float32),
            pltpu.VMEM((q_rows, HEAD_DIM), jnp.bfloat16),
            pltpu.VMEM((q_rows, HEAD_DIM), jnp.bfloat16),
            pltpu.VMEM((HEAD_DIM, q_rows), jnp.float32),
            pltpu.VMEM((HEAD_DIM, q_rows), jnp.float32),
            pltpu.VMEM((kv_heads, keys_all, wide), jnp.float32),
            pltpu.VMEM((kv_heads, keys_all, wide), jnp.bfloat16),
            pltpu.VMEM((kv_heads, 2, keys_all, wide), jnp.bfloat16),
            pltpu.VMEM((kv_heads, longest * rows, wide), jnp.bfloat16),
            pltpu.VMEM((kv_heads, 2, longest * rows, wide), jnp.bfloat16),
            pltpu.SemaphoreType.DMA((kv_heads, n_ctx, 4)),
            pltpu.SemaphoreType.DMA((kv_heads, n_ctx)),
            pltpu.SemaphoreType.DMA((kv_heads, n_ctx)),
            pltpu.SemaphoreType.DMA((kv_heads, 2, n_ctx)),
            pltpu.SemaphoreType.DMA((kv_heads, longest)),
            pltpu.SemaphoreType.DMA((kv_heads, 2, longest)),
        ],
        compiler_params=pltpu.CompilerParams(
            collective_id=0, has_side_effects=True, vmem_limit_bytes=60 * 1024 * 1024
        ),
        name="attention_fwd_bwd",
    )(queries, keys, values, out_grad, order)
    return tuple(hand_out(results))


def solution(mesh):
    return jax.shard_map(
        functools.partial(on_device, mesh.shape["ctx"]),
        mesh=mesh,
        in_specs=(P("ctx", "head"), P("ctx", "head"), P("ctx", "head"), P("ctx", "head"), P()),
        out_specs=(P("ctx", "head"), P("ctx", "head"), P("ctx", "head"), P("ctx", "head")),
        check_vma=False,
    )
```

```python
import functools
import math

import jax
import jax.numpy as jnp
from jax import lax
from jax.experimental import pallas as pl
from jax.experimental.pallas import tpu as pltpu
from jax.sharding import PartitionSpec as P

HEADS = 32
KV_HEADS = 8
HEAD_DIM = 128
GROUP = HEADS // KV_HEADS
NEG = -1e30
MESH = pl.DeviceIdType.MESH

UP, DOWN = 0, 1


def line_lengths(n_ctx):
    n0 = 4 if n_ctx % 4 == 0 else 1
    return n0, n_ctx // n0


def dot_nt(a, b):
    return lax.dot_general(a, b, (((1,), (1,)), ((), ())), preferred_element_type=jnp.float32)


def dot_tn(a, b):
    return lax.dot_general(a, b, (((0,), (0,)), ((), ())), preferred_element_type=jnp.float32)


def dot_nn(a, b):
    return lax.dot_general(a, b, (((1,), (0,)), ((), ())), preferred_element_type=jnp.float32)


def kernel(
    n_ctx, kv_heads, rows, kinds,
    q_ref, k_ref, v_ref, g_ref, order_ref,
    att_ref, dq_ref, dk_ref, dv_ref,
    kv, bias, probs, qs, gs, att_t, dq_t, acc,
    send_s, recv_s, send_f, recv_f,
    ag_send, ag_recv, s_send, s_recv, f_send, f_recv,
):
    n0, n1 = line_lengths(n_ctx)
    me = lax.axis_index("ctx")
    i0, i1 = me // n1, me % n1
    span = rows // 2
    half_keys = n_ctx * span
    q_rows = GROUP * rows
    skip = q_rows // 2 // 128 * 128
    scale = 1.0 / math.sqrt(HEAD_DIM)
    to_exp2 = scale * math.log2(math.e)

    class Kind:
        def __init__(self, index):
            self.index = index
            first_is_0 = kinds[index] == 0
            self.nf, self.ns = (n0, n1) if first_is_0 else (n1, n0)
            self.f, self.s = (i0, i1) if first_is_0 else (i1, i0)
            self.first_is_0 = first_is_0

        def device(self, f, s):
            return f * n1 + s if self.first_is_0 else s * n1 + f

        def slot(self, f, s):
            return s * self.nf + f

        def neighbour(self, line, direction):
            step = 1 if direction == UP else -1
            if line == 0:
                return self.device(self.f + step, self.s)
            return self.device(self.f, self.s + step)

        def has(self, line, direction):
            x, n = (self.f, self.nf) if line == 0 else (self.s, self.ns)
            return x + 1 < n if direction == UP else x > 0

    kind_list = [Kind(i) for i in range(len(kinds))]

    def kind_of(h):
        return kind_list[1 if h % 4 == 1 else 0]

    def block(slot):
        return pl.ds(pl.multiple_of(slot * span, span), span)

    first_span, second_span = order_ref[2 * me], order_ref[2 * me + 1]
    low_first = first_span < second_span

    def sort_halves(a, b):
        return jnp.where(low_first, a, b), jnp.where(low_first, b, a)

    barrier = pltpu.get_barrier_semaphore()
    base = kind_list[0]
    for line in (0, 1):
        for direction in (UP, DOWN):
            @pl.when(base.has(line, direction))
            def _(line=line, direction=direction):
                pl.semaphore_signal(
                    barrier, inc=1, device_id={"ctx": base.neighbour(line, direction)},
                    device_id_type=MESH,
                )
    peers = sum(
        base.has(line, direction).astype(jnp.int32) for line in (0, 1) for direction in (UP, DOWN)
    )
    pl.semaphore_wait(barrier, peers)

    def ag_copy(h, slot, line, direction):
        kind = kind_of(h)
        return pltpu.make_async_remote_copy(
            src_ref=kv.at[h, :, block(slot)],
            dst_ref=kv.at[h, :, block(slot)],
            send_sem=ag_send.at[h, slot, 2 * line + direction],
            recv_sem=ag_recv.at[h, slot],
            device_id={"ctx": kind.neighbour(line, direction)},
            device_id_type=MESH,
        )

    def ag_stage(h, stage, op):
        kind = kind_of(h)
        nf, ns, f, s = kind.nf, kind.ns, kind.f, kind.s

        def push(slot, line, direction):
            @pl.when(kind.has(line, direction))
            def _():
                copy = ag_copy(h, slot, line, direction)
                if op == "go":
                    copy.start()
                else:
                    copy.wait_send()

        def arrived(slot):
            if op == "go":
                ag_copy(h, slot, 0, UP).wait_recv()

        if stage == 0:
            own = kind.slot(f, s)
            if op == "go":
                columns = pl.ds(h * HEAD_DIM, HEAD_DIM)
                for ref, lanes in ((k_ref, pl.ds(0, HEAD_DIM)), (v_ref, pl.ds(HEAD_DIM, HEAD_DIM))):
                    low, high = sort_halves(ref[0:span, columns], ref[span:, columns])
                    kv[h, 0, block(own), lanes] = low
                    kv[h, 1, block(own), lanes] = high
            for line in (0, 1):
                push(own, line, UP)
                push(own, line, DOWN)
        elif stage < nf:
            for origin, direction in ((f - stage, UP), (f + stage, DOWN)):
                @pl.when(jnp.logical_and(origin >= 0, origin < nf))
                def _(origin=origin, direction=direction):
                    slot = kind.slot(origin, s)
                    arrived(slot)
                    push(slot, 0, direction)
                    push(slot, 1, UP)
                    push(slot, 1, DOWN)
        else:
            d = stage - nf + 1
            for origin, direction in ((s - d, UP), (s + d, DOWN)):
                @pl.when(jnp.logical_and(origin >= 0, origin < ns))
                def _(origin=origin, direction=direction):
                    for from_f in range(nf):
                        slot = kind.slot(from_f, origin)
                        arrived(slot)
                        push(slot, 1, direction)

    def ag_stages(h):
        return kind_of(h).nf + kind_of(h).ns - 1

    def s_copy(h, slot, direction):
        kind = kind_of(h)
        return pltpu.make_async_remote_copy(
            src_ref=send_s.at[h, :, block(slot)],
            dst_ref=recv_s.at[h, direction, :, block(slot)],
            send_sem=s_send.at[h, slot],
            recv_sem=s_recv.at[h, direction, slot],
            device_id={"ctx": kind.device(kind.f, kind.s + 1 - 2 * direction)},
            device_id_type=MESH,
        )

    def f_copy(h, x, direction):
        kind = kind_of(h)
        return pltpu.make_async_remote_copy(
            src_ref=send_f.at[h, :, block(x)],
            dst_ref=recv_f.at[h, direction, :, block(x)],
            send_sem=f_send.at[h, x],
            recv_sem=f_recv.at[h, direction, x],
            device_id={"ctx": kind.neighbour(0, direction)},
            device_id_type=MESH,
        )

    def s_pass_on(h, slot, direction, first):
        total = acc[h, :, block(slot)]
        copy = s_copy(h, slot, direction)
        if not first:
            copy.wait_recv()
            total = total + recv_s[h, direction, :, block(slot)].astype(jnp.float32)
        send_s[h, :, block(slot)] = total.astype(jnp.bfloat16)
        copy.start()

    def s_stage(h, stage):
        kind = kind_of(h)
        n = kind.ns

        @pl.when(kind.s == stage)
        def _():
            for x in range(n - 1, stage, -1):
                for f in range(kind.nf):
                    s_pass_on(h, kind.slot(f, x), UP, False)

        @pl.when(kind.s == n - 1 - stage)
        def _():
            for x in range(0, n - 1 - stage):
                for f in range(kind.nf):
                    s_pass_on(h, kind.slot(f, x), DOWN, False)

    def take_s(h, slot):
        kind = kind_of(h)
        for direction, there in ((UP, kind.s > 0), (DOWN, kind.s < kind.ns - 1)):
            @pl.when(there)
            def _(direction=direction):
                s_copy(h, slot, direction).wait_recv()
                where = block(slot)
                acc[h, :, where] = acc[h, :, where] + recv_s[h, direction, :, where].astype(jnp.float32)

    def f_stage(h, stage):
        kind = kind_of(h)
        n = kind.nf

        def pass_on(x, direction):
            slot = kind.slot(x, kind.s)
            take_s(h, slot)
            total = acc[h, :, block(slot)]
            copy = f_copy(h, x, direction)
            if stage > 0:
                copy.wait_recv()
                total = total + recv_f[h, direction, :, block(x)].astype(jnp.float32)
            send_f[h, :, block(x)] = total.astype(jnp.bfloat16)
            copy.start()

        @pl.when(kind.f == stage)
        def _():
            for x in range(n - 1, stage, -1):
                pass_on(x, UP)

        @pl.when(kind.f == n - 1 - stage)
        def _():
            for x in range(0, n - 1 - stage):
                pass_on(x, DOWN)

    def finish(h):
        kind = kind_of(h)
        own = kind.slot(kind.f, kind.s)
        take_s(h, own)
        where = block(own)
        for direction, there in ((UP, kind.f > 0), (DOWN, kind.f < kind.nf - 1)):
            @pl.when(there)
            def _(direction=direction):
                f_copy(h, kind.f, direction).wait_recv()
                acc[h, :, where] = acc[h, :, where] + recv_f[
                    h, direction, :, block(kind.f)
                ].astype(jnp.float32)
        columns = pl.ds(h * HEAD_DIM, HEAD_DIM)
        both = sort_halves(acc[h, 0, where], acc[h, 1, where])
        for i in range(2):
            rows_here = pl.ds(i * span, span)
            dk_ref[rows_here, columns] = (both[i][:, :HEAD_DIM] * scale).astype(jnp.bfloat16)
            dv_ref[rows_here, columns] = both[i][:, HEAD_DIM:].astype(jnp.bfloat16)

    def rs_tasks(h):
        kind = kind_of(h)
        tasks = [functools.partial(s_stage, h, stage) for stage in range(1, kind.ns - 1)]
        tasks += [functools.partial(f_stage, h, stage) for stage in range(kind.nf - 1)]
        return tasks + [functools.partial(finish, h)]

    def make_bias(kind):
        lane = lax.broadcasted_iota(jnp.int32, (1, q_rows), 1)
        low = jnp.minimum(first_span, second_span) * span
        high = jnp.maximum(first_span, second_span) * span
        q_pos = lane % span + jnp.where(lane < GROUP * span, low, high)
        row = lax.broadcasted_iota(jnp.int32, (span, q_rows), 0)

        @pl.loop(0, n_ctx)
        def _(slot):
            source = kind.device(slot % kind.nf, slot // kind.nf)
            a, b = order_ref[2 * source], order_ref[2 * source + 1]
            for half, start in ((0, jnp.minimum(a, b)), (1, jnp.maximum(a, b))):
                visible = row + start * span <= q_pos
                bias[kind.index, half, block(slot)] = jnp.where(visible, 0.0, NEG)

    halves = ((0, 0), (1, skip))

    def load_queries(h):
        for g in range(GROUP):
            columns = pl.ds((h * GROUP + g) * HEAD_DIM, HEAD_DIM)
            for ref, to in ((q_ref, qs), (g_ref, gs)):
                low, high = sort_halves(ref[0:span, columns], ref[span:, columns])
                to[pl.ds(g * span, span)] = low
                to[pl.ds((GROUP + g) * span, span)] = high

    def write_rows(ref, h, result):
        for g in range(GROUP):
            columns = pl.ds((h * GROUP + g) * HEAD_DIM, HEAD_DIM)
            first, second = sort_halves(
                result[g * span:(g + 1) * span],
                result[(GROUP + g) * span:(GROUP + g + 1) * span],
            )
            ref[0:span, columns] = first
            ref[span:, columns] = second

    def rows_of(i, size):
        return pl.ds(pl.multiple_of(i * size, size), size)

    tall = min(half_keys, 4 * span)

    def fold(x, op):
        return op(x.reshape(x.shape[0] // 8, 8, x.shape[1]), axis=0)

    def join(parts, op):
        low, high = (op(x, axis=0, keepdims=True) for x in parts)
        both = op(jnp.concatenate([low[:, skip:], high], axis=0), axis=0, keepdims=True)
        return jnp.concatenate([low[:, :skip], both], axis=1)

    def scores_pass(h):
        kind = kind_of(h)

        def body(i, tops):
            where = rows_of(i, tall)
            out = []
            for half, lanes in halves:
                s = dot_nt(kv[h, half, where, 0:HEAD_DIM], qs[lanes:])
                s = s + bias[kind.index, half, where, lanes:]
                probs[half, where, lanes:] = s
                out.append(jnp.maximum(tops[half], fold(s, jnp.max)))
            return tuple(out)

        tops = lax.fori_loop(
            0, half_keys // tall, body,
            tuple(jnp.full((8, q_rows - lanes), NEG, jnp.float32) for _, lanes in halves),
        )
        return join(tops, jnp.max) * to_exp2

    def weights_pass(h, top):
        att_t[...] = jnp.zeros_like(att_t)

        def body(i, totals):
            where = rows_of(i, tall)
            out = []
            for half, lanes in halves:
                e = jnp.exp2(probs[half, where, lanes:] * to_exp2 - top[:, lanes:])
                probs[half, where, lanes:] = e
                att_t[:, lanes:] += dot_tn(kv[h, half, where, HEAD_DIM:], e.astype(jnp.bfloat16))
                out.append(totals[half] + fold(e, jnp.sum))
            return tuple(out)

        totals = lax.fori_loop(
            0, half_keys // tall, body,
            tuple(jnp.zeros((8, q_rows - lanes), jnp.float32) for _, lanes in halves),
        )
        inverse = 1.0 / join(totals, jnp.sum)
        attention = (att_t[...] * inverse).T.astype(jnp.bfloat16)
        write_rows(att_ref, h, attention)
        product = gs[...].astype(jnp.float32) * attention.astype(jnp.float32)
        row_dot = jnp.sum(product.T, axis=0, keepdims=True)
        return inverse, row_dot

    def backward_group(h, s, inverse, row_dot, send):
        kind = kind_of(h)
        where = rows_of(s, kind.nf * span)
        for half, lanes in halves:
            k, v = kv[h, half, where, 0:HEAD_DIM], kv[h, half, where, HEAD_DIM:]
            p = probs[half, where, lanes:] * inverse[:, lanes:]
            ds = (p * (dot_nt(v, gs[lanes:]) - row_dot[:, lanes:])).astype(jnp.bfloat16)
            acc[h, half, where, 0:HEAD_DIM] = dot_nn(ds, qs[lanes:])
            acc[h, half, where, HEAD_DIM:] = dot_nn(p.astype(jnp.bfloat16), gs[lanes:])
            dq_t[:, lanes:] += dot_tn(k, ds)
        if send:
            direction = jnp.where(s > kind.s, UP, DOWN)
            first = jnp.logical_or(
                jnp.logical_and(s > kind.s, kind.s == 0),
                jnp.logical_and(s < kind.s, kind.s == kind.ns - 1),
            )
            backwards = kind.f < kind.nf // 2

            @pl.when(first)
            def _():
                for b in range(kind.nf):
                    b = jnp.where(backwards, kind.nf - 1 - b, b)
                    s_pass_on(h, s * kind.nf + b, direction, True)

    def write_dq(h):
        write_rows(dq_ref, h, (dq_t[...] * scale).T.astype(jnp.bfloat16))

    lag = 2
    ticks = []
    last_tick = lag * (kv_heads - 1) + max(ag_stages(h) for h in range(kv_heads))
    for t in range(last_tick):
        ticks.append([
            (h, t - lag * h) for h in range(kv_heads) if 0 <= t - lag * h < ag_stages(h)
        ])
    done = 0

    def run_ticks(until):
        nonlocal done
        while done < min(until, len(ticks)):
            for h, stage in ticks[done]:
                ag_stage(h, stage, "go")
            done += 1

    chains = []

    def advance():
        for chain in list(chains):
            chain.pop(0)()
            if not chain:
                chains.remove(chain)

    run_ticks(1)
    for kind in kind_list:
        make_bias(kind)
    load_queries(0)
    for h in range(kv_heads):
        kind = kind_of(h)
        run_ticks(lag * h + ag_stages(h))
        if h:
            load_queries(h)
        top = scores_pass(h)
        run_ticks(lag * h + ag_stages(h) + 1)
        inverse, row_dot = weights_pass(h, top)
        run_ticks(lag * h + ag_stages(h) + 2)
        advance()
        dq_t[...] = jnp.zeros_like(dq_t)

        def away(j, _):
            backward_group(h, lax.rem(kind.s + j, kind.ns), inverse, row_dot, True)
            return 0

        lax.fori_loop(1, kind.ns, away, 0)
        backward_group(h, kind.s, inverse, row_dot, False)
        advance()
        chains.append(rs_tasks(h))
        if h == kv_heads - 1:
            advance()
        write_dq(h)
    while chains:
        advance()

    for h in range(kv_heads):
        kind = kind_of(h)
        for stage in range(ag_stages(h)):
            ag_stage(h, stage, "sent")

        def sent(j, _):
            group = lax.rem(kind.s + j, kind.ns)
            for f in range(kind.nf):
                s_copy(h, kind.slot(f, group), UP).wait_send()
            return 0

        lax.fori_loop(1, kind.ns, sent, 0)
        for j in range(1, kind.nf):
            f_copy(h, lax.rem(kind.f + j, kind.nf), UP).wait_send()


def copy_kernel(*refs):
    sems = refs[-1]
    count = (len(refs) - 1) // 2
    copies = [
        pltpu.make_async_copy(refs[i], refs[count + i], sems.at[i]) for i in range(count)
    ]
    for copy in copies:
        copy.start()
    for copy in copies:
        copy.wait()


def hand_out(results):
    anywhere = pl.BlockSpec(memory_space=pl.ANY)
    return pl.pallas_call(
        copy_kernel,
        out_shape=[jax.ShapeDtypeStruct(x.shape, x.dtype) for x in results],
        in_specs=[pl.BlockSpec(memory_space=pltpu.VMEM)] * len(results),
        out_specs=[anywhere] * len(results),
        scratch_shapes=[pltpu.SemaphoreType.DMA((len(results),))],
        name="hand_out",
    )(*results)


def on_device(n_ctx, queries, keys, values, out_grad, order):
    rows = queries.shape[0]
    kv_heads = keys.shape[1] // HEAD_DIM
    q_rows = GROUP * rows
    half_keys = n_ctx * rows // 2
    n0, n1 = line_lengths(n_ctx)
    kinds = (0, 1) if kv_heads > 1 else (0,)
    wide = 2 * HEAD_DIM
    longest = max(n0, n1)
    vmem = pl.BlockSpec(memory_space=pltpu.VMEM)
    results = pl.pallas_call(
        functools.partial(kernel, n_ctx, kv_heads, rows, kinds),
        out_shape=[
            jax.ShapeDtypeStruct(x.shape, jnp.bfloat16) for x in (queries, queries, keys, values)
        ],
        in_specs=[vmem] * 4 + [pl.BlockSpec(memory_space=pltpu.SMEM)],
        out_specs=[vmem] * 4,
        scratch_shapes=[
            pltpu.VMEM((kv_heads, 2, half_keys, wide), jnp.bfloat16),
            pltpu.VMEM((len(kinds), 2, half_keys, q_rows), jnp.float32),
            pltpu.VMEM((2, half_keys, q_rows), jnp.float32),
            pltpu.VMEM((q_rows, HEAD_DIM), jnp.bfloat16),
            pltpu.VMEM((q_rows, HEAD_DIM), jnp.bfloat16),
            pltpu.VMEM((HEAD_DIM, q_rows), jnp.float32),
            pltpu.VMEM((HEAD_DIM, q_rows), jnp.float32),
            pltpu.VMEM((kv_heads, 2, half_keys, wide), jnp.float32),
            pltpu.VMEM((kv_heads, 2, half_keys, wide), jnp.bfloat16),
            pltpu.VMEM((kv_heads, 2, 2, half_keys, wide), jnp.bfloat16),
            pltpu.VMEM((kv_heads, 2, longest * rows // 2, wide), jnp.bfloat16),
            pltpu.VMEM((kv_heads, 2, 2, longest * rows // 2, wide), jnp.bfloat16),
            pltpu.SemaphoreType.DMA((kv_heads, n_ctx, 4)),
            pltpu.SemaphoreType.DMA((kv_heads, n_ctx)),
            pltpu.SemaphoreType.DMA((kv_heads, n_ctx)),
            pltpu.SemaphoreType.DMA((kv_heads, 2, n_ctx)),
            pltpu.SemaphoreType.DMA((kv_heads, longest)),
            pltpu.SemaphoreType.DMA((kv_heads, 2, longest)),
        ],
        compiler_params=pltpu.CompilerParams(
            collective_id=0, has_side_effects=True, vmem_limit_bytes=60 * 1024 * 1024
        ),
        name="attention_fwd_bwd",
    )(queries, keys, values, out_grad, order)
    return tuple(hand_out(results))


def solution(mesh):
    return jax.shard_map(
        functools.partial(on_device, mesh.shape["ctx"]),
        mesh=mesh,
        in_specs=(P("ctx", "head"), P("ctx", "head"), P("ctx", "head"), P("ctx", "head"), P()),
        out_specs=(P("ctx", "head"), P("ctx", "head"), P("ctx", "head"), P("ctx", "head")),
        check_vma=False,
    )
```

```python
import functools
import math

import jax
import jax.numpy as jnp
from jax import lax
from jax.experimental import pallas as pl
from jax.experimental.pallas import tpu as pltpu
from jax.sharding import PartitionSpec as P

HEADS = 32
KV_HEADS = 8
HEAD_DIM = 128
GROUP = HEADS // KV_HEADS
NEG = -1e30
MESH = pl.DeviceIdType.MESH

UP, DOWN = 0, 1


def line_lengths(n_ctx):
    n0 = 4 if n_ctx % 4 == 0 else 1
    return n0, n_ctx // n0


def dot_nt(a, b):
    return lax.dot_general(a, b, (((1,), (1,)), ((), ())), preferred_element_type=jnp.float32)


def dot_tn(a, b):
    return lax.dot_general(a, b, (((0,), (0,)), ((), ())), preferred_element_type=jnp.float32)


def dot_nn(a, b):
    return lax.dot_general(a, b, (((1,), (0,)), ((), ())), preferred_element_type=jnp.float32)


def kernel(
    n_ctx, kv_heads, rows, kinds,
    q_ref, k_ref, v_ref, g_ref, order_ref,
    att_ref, dq_ref, dk_ref, dv_ref,
    kv, bias, probs, qs, gs, att_t, dq_t, acc,
    send_s, recv_s, send_f, recv_f,
    ag_send, ag_recv, s_send, s_recv, f_send, f_recv,
):
    n0, n1 = line_lengths(n_ctx)
    me = lax.axis_index("ctx")
    i0, i1 = me // n1, me % n1
    span = rows // 2
    half_keys = n_ctx * span
    q_rows = GROUP * rows
    skip = q_rows // 2 // 128 * 128
    scale = 1.0 / math.sqrt(HEAD_DIM)
    to_exp2 = scale * math.log2(math.e)

    class Kind:
        def __init__(self, index):
            self.index = index
            first_is_0 = kinds[index] == 0
            self.nf, self.ns = (n0, n1) if first_is_0 else (n1, n0)
            self.f, self.s = (i0, i1) if first_is_0 else (i1, i0)
            self.first_is_0 = first_is_0

        def device(self, f, s):
            return f * n1 + s if self.first_is_0 else s * n1 + f

        def slot(self, f, s):
            return s * self.nf + f

        def neighbour(self, line, direction):
            step = 1 if direction == UP else -1
            if line == 0:
                return self.device(self.f + step, self.s)
            return self.device(self.f, self.s + step)

        def has(self, line, direction):
            x, n = (self.f, self.nf) if line == 0 else (self.s, self.ns)
            return x + 1 < n if direction == UP else x > 0

    kind_list = [Kind(i) for i in range(len(kinds))]

    def kind_of(h):
        return kind_list[h % len(kinds)]

    def block(slot):
        return pl.ds(pl.multiple_of(slot * span, span), span)

    first_span, second_span = order_ref[2 * me], order_ref[2 * me + 1]
    low_first = first_span < second_span

    def sort_halves(a, b):
        return jnp.where(low_first, a, b), jnp.where(low_first, b, a)

    barrier = pltpu.get_barrier_semaphore()
    base = kind_list[0]
    for line in (0, 1):
        for direction in (UP, DOWN):
            @pl.when(base.has(line, direction))
            def _(line=line, direction=direction):
                pl.semaphore_signal(
                    barrier, inc=1, device_id={"ctx": base.neighbour(line, direction)},
                    device_id_type=MESH,
                )
    peers = sum(
        base.has(line, direction).astype(jnp.int32) for line in (0, 1) for direction in (UP, DOWN)
    )
    pl.semaphore_wait(barrier, peers)

    def ag_copy(h, slot, line, direction):
        kind = kind_of(h)
        return pltpu.make_async_remote_copy(
            src_ref=kv.at[h, :, block(slot)],
            dst_ref=kv.at[h, :, block(slot)],
            send_sem=ag_send.at[h, slot, 2 * line + direction],
            recv_sem=ag_recv.at[h, slot],
            device_id={"ctx": kind.neighbour(line, direction)},
            device_id_type=MESH,
        )

    def ag_stage(h, stage, op):
        kind = kind_of(h)
        nf, ns, f, s = kind.nf, kind.ns, kind.f, kind.s

        def push(slot, line, direction):
            @pl.when(kind.has(line, direction))
            def _():
                copy = ag_copy(h, slot, line, direction)
                if op == "go":
                    copy.start()
                else:
                    copy.wait_send()

        def arrived(slot):
            if op == "go":
                ag_copy(h, slot, 0, UP).wait_recv()

        if stage == 0:
            own = kind.slot(f, s)
            if op == "go":
                columns = pl.ds(h * HEAD_DIM, HEAD_DIM)
                for ref, lanes in ((k_ref, pl.ds(0, HEAD_DIM)), (v_ref, pl.ds(HEAD_DIM, HEAD_DIM))):
                    low, high = sort_halves(ref[0:span, columns], ref[span:, columns])
                    kv[h, 0, block(own), lanes] = low
                    kv[h, 1, block(own), lanes] = high
            for line in (0, 1):
                push(own, line, UP)
                push(own, line, DOWN)
        elif stage < nf:
            for origin, direction in ((f - stage, UP), (f + stage, DOWN)):
                @pl.when(jnp.logical_and(origin >= 0, origin < nf))
                def _(origin=origin, direction=direction):
                    slot = kind.slot(origin, s)
                    arrived(slot)
                    push(slot, 0, direction)
                    push(slot, 1, UP)
                    push(slot, 1, DOWN)
        else:
            d = stage - nf + 1
            for origin, direction in ((s - d, UP), (s + d, DOWN)):
                @pl.when(jnp.logical_and(origin >= 0, origin < ns))
                def _(origin=origin, direction=direction):
                    for from_f in range(nf):
                        slot = kind.slot(from_f, origin)
                        arrived(slot)
                        push(slot, 1, direction)

    def ag_stages(h):
        return kind_of(h).nf + kind_of(h).ns - 1

    def s_copy(h, slot, direction):
        kind = kind_of(h)
        return pltpu.make_async_remote_copy(
            src_ref=send_s.at[h, :, block(slot)],
            dst_ref=recv_s.at[h, direction, :, block(slot)],
            send_sem=s_send.at[h, slot],
            recv_sem=s_recv.at[h, direction, slot],
            device_id={"ctx": kind.device(kind.f, kind.s + 1 - 2 * direction)},
            device_id_type=MESH,
        )

    def f_copy(h, x, direction):
        kind = kind_of(h)
        return pltpu.make_async_remote_copy(
            src_ref=send_f.at[h, :, block(x)],
            dst_ref=recv_f.at[h, direction, :, block(x)],
            send_sem=f_send.at[h, x],
            recv_sem=f_recv.at[h, direction, x],
            device_id={"ctx": kind.neighbour(0, direction)},
            device_id_type=MESH,
        )

    def s_pass_on(h, slot, direction, first):
        total = acc[h, :, block(slot)]
        copy = s_copy(h, slot, direction)
        if not first:
            copy.wait_recv()
            total = total + recv_s[h, direction, :, block(slot)].astype(jnp.float32)
        send_s[h, :, block(slot)] = total.astype(jnp.bfloat16)
        copy.start()

    def s_stage(h, stage):
        kind = kind_of(h)
        n = kind.ns

        @pl.when(kind.s == stage)
        def _():
            for x in range(n - 1, stage, -1):
                for f in range(kind.nf):
                    s_pass_on(h, kind.slot(f, x), UP, False)

        @pl.when(kind.s == n - 1 - stage)
        def _():
            for x in range(0, n - 1 - stage):
                for f in range(kind.nf):
                    s_pass_on(h, kind.slot(f, x), DOWN, False)

    def take_s(h, slot):
        kind = kind_of(h)
        for direction, there in ((UP, kind.s > 0), (DOWN, kind.s < kind.ns - 1)):
            @pl.when(there)
            def _(direction=direction):
                s_copy(h, slot, direction).wait_recv()
                where = block(slot)
                acc[h, :, where] = acc[h, :, where] + recv_s[h, direction, :, where].astype(jnp.float32)

    def f_stage(h, stage):
        kind = kind_of(h)
        n = kind.nf

        def pass_on(x, direction):
            slot = kind.slot(x, kind.s)
            take_s(h, slot)
            total = acc[h, :, block(slot)]
            copy = f_copy(h, x, direction)
            if stage > 0:
                copy.wait_recv()
                total = total + recv_f[h, direction, :, block(x)].astype(jnp.float32)
            send_f[h, :, block(x)] = total.astype(jnp.bfloat16)
            copy.start()

        @pl.when(kind.f == stage)
        def _():
            for x in range(n - 1, stage, -1):
                pass_on(x, UP)

        @pl.when(kind.f == n - 1 - stage)
        def _():
            for x in range(0, n - 1 - stage):
                pass_on(x, DOWN)

    def finish(h):
        kind = kind_of(h)
        own = kind.slot(kind.f, kind.s)
        take_s(h, own)
        where = block(own)
        for direction, there in ((UP, kind.f > 0), (DOWN, kind.f < kind.nf - 1)):
            @pl.when(there)
            def _(direction=direction):
                f_copy(h, kind.f, direction).wait_recv()
                acc[h, :, where] = acc[h, :, where] + recv_f[
                    h, direction, :, block(kind.f)
                ].astype(jnp.float32)
        columns = pl.ds(h * HEAD_DIM, HEAD_DIM)
        both = sort_halves(acc[h, 0, where], acc[h, 1, where])
        for i in range(2):
            rows_here = pl.ds(i * span, span)
            dk_ref[rows_here, columns] = (both[i][:, :HEAD_DIM] * scale).astype(jnp.bfloat16)
            dv_ref[rows_here, columns] = both[i][:, HEAD_DIM:].astype(jnp.bfloat16)

    def rs_tasks(h):
        kind = kind_of(h)
        tasks = [functools.partial(s_stage, h, stage) for stage in range(1, kind.ns - 1)]
        tasks += [functools.partial(f_stage, h, stage) for stage in range(kind.nf - 1)]
        return tasks + [functools.partial(finish, h)]

    def make_bias(kind):
        lane = lax.broadcasted_iota(jnp.int32, (1, q_rows), 1)
        low = jnp.minimum(first_span, second_span) * span
        high = jnp.maximum(first_span, second_span) * span
        q_pos = lane % span + jnp.where(lane < GROUP * span, low, high)
        row = lax.broadcasted_iota(jnp.int32, (span, q_rows), 0)

        @pl.loop(0, n_ctx)
        def _(slot):
            source = kind.device(slot % kind.nf, slot // kind.nf)
            a, b = order_ref[2 * source], order_ref[2 * source + 1]
            for half, start in ((0, jnp.minimum(a, b)), (1, jnp.maximum(a, b))):
                visible = row + start * span <= q_pos
                bias[kind.index, half, block(slot)] = jnp.where(visible, 0.0, NEG)

    halves = ((0, 0), (1, skip))

    def load_queries(h):
        for g in range(GROUP):
            columns = pl.ds((h * GROUP + g) * HEAD_DIM, HEAD_DIM)
            for ref, to in ((q_ref, qs), (g_ref, gs)):
                low, high = sort_halves(ref[0:span, columns], ref[span:, columns])
                to[pl.ds(g * span, span)] = low
                to[pl.ds((GROUP + g) * span, span)] = high

    def write_rows(ref, h, result):
        for g in range(GROUP):
            columns = pl.ds((h * GROUP + g) * HEAD_DIM, HEAD_DIM)
            first, second = sort_halves(
                result[g * span:(g + 1) * span],
                result[(GROUP + g) * span:(GROUP + g + 1) * span],
            )
            ref[0:span, columns] = first
            ref[span:, columns] = second

    def rows_of(i, size):
        return pl.ds(pl.multiple_of(i * size, size), size)

    tall = min(half_keys, 4 * span)

    def fold(x, op):
        return op(x.reshape(x.shape[0] // 8, 8, x.shape[1]), axis=0)

    def join(parts, op):
        low, high = (op(x, axis=0, keepdims=True) for x in parts)
        both = op(jnp.concatenate([low[:, skip:], high], axis=0), axis=0, keepdims=True)
        return jnp.concatenate([low[:, :skip], both], axis=1)

    def scores_pass(h):
        kind = kind_of(h)

        def body(i, tops):
            where = rows_of(i, tall)
            out = []
            for half, lanes in halves:
                s = dot_nt(kv[h, half, where, 0:HEAD_DIM], qs[lanes:])
                s = s + bias[kind.index, half, where, lanes:]
                probs[half, where, lanes:] = s
                out.append(jnp.maximum(tops[half], fold(s, jnp.max)))
            return tuple(out)

        tops = lax.fori_loop(
            0, half_keys // tall, body,
            tuple(jnp.full((8, q_rows - lanes), NEG, jnp.float32) for _, lanes in halves),
        )
        return join(tops, jnp.max) * to_exp2

    def weights_pass(h, top):
        att_t[...] = jnp.zeros_like(att_t)

        def body(i, totals):
            where = rows_of(i, tall)
            out = []
            for half, lanes in halves:
                e = jnp.exp2(probs[half, where, lanes:] * to_exp2 - top[:, lanes:])
                probs[half, where, lanes:] = e
                att_t[:, lanes:] += dot_tn(kv[h, half, where, HEAD_DIM:], e.astype(jnp.bfloat16))
                out.append(totals[half] + fold(e, jnp.sum))
            return tuple(out)

        totals = lax.fori_loop(
            0, half_keys // tall, body,
            tuple(jnp.zeros((8, q_rows - lanes), jnp.float32) for _, lanes in halves),
        )
        inverse = 1.0 / join(totals, jnp.sum)
        attention = (att_t[...] * inverse).T.astype(jnp.bfloat16)
        write_rows(att_ref, h, attention)
        product = gs[...].astype(jnp.float32) * attention.astype(jnp.float32)
        row_dot = jnp.sum(product.T, axis=0, keepdims=True)
        return inverse, row_dot

    def backward_group(h, s, inverse, row_dot, send):
        kind = kind_of(h)
        where = rows_of(s, kind.nf * span)
        for half, lanes in halves:
            k, v = kv[h, half, where, 0:HEAD_DIM], kv[h, half, where, HEAD_DIM:]
            p = probs[half, where, lanes:] * inverse[:, lanes:]
            ds = (p * (dot_nt(v, gs[lanes:]) - row_dot[:, lanes:])).astype(jnp.bfloat16)
            acc[h, half, where, 0:HEAD_DIM] = dot_nn(ds, qs[lanes:])
            acc[h, half, where, HEAD_DIM:] = dot_nn(p.astype(jnp.bfloat16), gs[lanes:])
            dq_t[:, lanes:] += dot_tn(k, ds)
        if send:
            direction = jnp.where(s > kind.s, UP, DOWN)
            first = jnp.logical_or(
                jnp.logical_and(s > kind.s, kind.s == 0),
                jnp.logical_and(s < kind.s, kind.s == kind.ns - 1),
            )
            backwards = kind.f < kind.nf // 2

            @pl.when(first)
            def _():
                for b in range(kind.nf):
                    b = jnp.where(backwards, kind.nf - 1 - b, b)
                    s_pass_on(h, s * kind.nf + b, direction, True)

    def write_dq(h):
        write_rows(dq_ref, h, (dq_t[...] * scale).T.astype(jnp.bfloat16))

    lag = 1
    ticks = []
    last_tick = lag * (kv_heads - 1) + max(ag_stages(h) for h in range(kv_heads))
    for t in range(last_tick):
        ticks.append([
            (h, t - lag * h) for h in range(kv_heads) if 0 <= t - lag * h < ag_stages(h)
        ])
    done = 0

    def run_ticks(until):
        nonlocal done
        while done < min(until, len(ticks)):
            for h, stage in ticks[done]:
                ag_stage(h, stage, "go")
            done += 1

    chains = []

    def advance():
        for chain in list(chains):
            chain.pop(0)()
            if not chain:
                chains.remove(chain)

    run_ticks(1)
    for kind in kind_list:
        make_bias(kind)
    load_queries(0)
    for h in range(kv_heads):
        kind = kind_of(h)
        run_ticks(lag * h + ag_stages(h))
        if h:
            load_queries(h)
        top = scores_pass(h)
        run_ticks(done + 1)
        inverse, row_dot = weights_pass(h, top)
        run_ticks(done + 1)
        advance()
        dq_t[...] = jnp.zeros_like(dq_t)

        def away(j, _):
            backward_group(h, lax.rem(kind.s + j, kind.ns), inverse, row_dot, True)
            return 0

        lax.fori_loop(1, kind.ns, away, 0)
        run_ticks(done + 1)
        backward_group(h, kind.s, inverse, row_dot, False)
        advance()
        chains.append(rs_tasks(h))
        if h == kv_heads - 1:
            advance()
        write_dq(h)
    while chains:
        advance()

    for h in range(kv_heads):
        kind = kind_of(h)
        for stage in range(ag_stages(h)):
            ag_stage(h, stage, "sent")

        def sent(j, _):
            group = lax.rem(kind.s + j, kind.ns)
            for f in range(kind.nf):
                s_copy(h, kind.slot(f, group), UP).wait_send()
            return 0

        lax.fori_loop(1, kind.ns, sent, 0)
        for j in range(1, kind.nf):
            f_copy(h, lax.rem(kind.f + j, kind.nf), UP).wait_send()


def copy_kernel(*refs):
    sems = refs[-1]
    count = (len(refs) - 1) // 2
    copies = [
        pltpu.make_async_copy(refs[i], refs[count + i], sems.at[i]) for i in range(count)
    ]
    for copy in copies:
        copy.start()
    for copy in copies:
        copy.wait()


def hand_out(results):
    anywhere = pl.BlockSpec(memory_space=pl.ANY)
    return pl.pallas_call(
        copy_kernel,
        out_shape=[jax.ShapeDtypeStruct(x.shape, x.dtype) for x in results],
        in_specs=[pl.BlockSpec(memory_space=pltpu.VMEM)] * len(results),
        out_specs=[anywhere] * len(results),
        scratch_shapes=[pltpu.SemaphoreType.DMA((len(results),))],
        name="hand_out",
    )(*results)


def on_device(n_ctx, queries, keys, values, out_grad, order):
    rows = queries.shape[0]
    kv_heads = keys.shape[1] // HEAD_DIM
    q_rows = GROUP * rows
    half_keys = n_ctx * rows // 2
    n0, n1 = line_lengths(n_ctx)
    kinds = (0,)
    wide = 2 * HEAD_DIM
    longest = max(n0, n1)
    vmem = pl.BlockSpec(memory_space=pltpu.VMEM)
    results = pl.pallas_call(
        functools.partial(kernel, n_ctx, kv_heads, rows, kinds),
        out_shape=[
            jax.ShapeDtypeStruct(x.shape, jnp.bfloat16) for x in (queries, queries, keys, values)
        ],
        in_specs=[vmem] * 4 + [pl.BlockSpec(memory_space=pltpu.SMEM)],
        out_specs=[vmem] * 4,
        scratch_shapes=[
            pltpu.VMEM((kv_heads, 2, half_keys, wide), jnp.bfloat16),
            pltpu.VMEM((len(kinds), 2, half_keys, q_rows), jnp.float32),
            pltpu.VMEM((2, half_keys, q_rows), jnp.float32),
            pltpu.VMEM((q_rows, HEAD_DIM), jnp.bfloat16),
            pltpu.VMEM((q_rows, HEAD_DIM), jnp.bfloat16),
            pltpu.VMEM((HEAD_DIM, q_rows), jnp.float32),
            pltpu.VMEM((HEAD_DIM, q_rows), jnp.float32),
            pltpu.VMEM((kv_heads, 2, half_keys, wide), jnp.float32),
            pltpu.VMEM((kv_heads, 2, half_keys, wide), jnp.bfloat16),
            pltpu.VMEM((kv_heads, 2, 2, half_keys, wide), jnp.bfloat16),
            pltpu.VMEM((kv_heads, 2, longest * rows // 2, wide), jnp.bfloat16),
            pltpu.VMEM((kv_heads, 2, 2, longest * rows // 2, wide), jnp.bfloat16),
            pltpu.SemaphoreType.DMA((kv_heads, n_ctx, 4)),
            pltpu.SemaphoreType.DMA((kv_heads, n_ctx)),
            pltpu.SemaphoreType.DMA((kv_heads, n_ctx)),
            pltpu.SemaphoreType.DMA((kv_heads, 2, n_ctx)),
            pltpu.SemaphoreType.DMA((kv_heads, longest)),
            pltpu.SemaphoreType.DMA((kv_heads, 2, longest)),
        ],
        compiler_params=pltpu.CompilerParams(
            collective_id=0, has_side_effects=True, vmem_limit_bytes=60 * 1024 * 1024
        ),
        name="attention_fwd_bwd",
    )(queries, keys, values, out_grad, order)
    return tuple(hand_out(results))


def solution(mesh):
    return jax.shard_map(
        functools.partial(on_device, mesh.shape["ctx"]),
        mesh=mesh,
        in_specs=(P("ctx", "head"), P("ctx", "head"), P("ctx", "head"), P("ctx", "head"), P()),
        out_specs=(P("ctx", "head"), P("ctx", "head"), P("ctx", "head"), P("ctx", "head")),
        check_vma=False,
    )
```

```python
import functools
import math

import jax
import jax.numpy as jnp
from jax import lax
from jax.experimental import pallas as pl
from jax.experimental.pallas import tpu as pltpu
from jax.sharding import PartitionSpec as P

HEADS = 32
KV_HEADS = 8
HEAD_DIM = 128
GROUP = HEADS // KV_HEADS
NEG = -1e30
MESH = pl.DeviceIdType.MESH

UP, DOWN = 0, 1


def line_lengths(n_ctx):
    n0 = 4 if n_ctx % 4 == 0 else 1
    return n0, n_ctx // n0


def dot_nt(a, b):
    return lax.dot_general(a, b, (((1,), (1,)), ((), ())), preferred_element_type=jnp.float32)


def dot_tn(a, b):
    return lax.dot_general(a, b, (((0,), (0,)), ((), ())), preferred_element_type=jnp.float32)


def dot_nn(a, b):
    return lax.dot_general(a, b, (((1,), (0,)), ((), ())), preferred_element_type=jnp.float32)


def kernel(
    n_ctx, kv_heads, rows, kinds,
    q_ref, k_ref, v_ref, g_ref, order_ref,
    att_ref, dq_ref, dk_ref, dv_ref,
    kv, bias, probs, qs, gs, att_t, dq_t, acc,
    send_s, recv_s, send_f, recv_f,
    ag_send, ag_recv, s_send, s_recv, f_send, f_recv,
):
    n0, n1 = line_lengths(n_ctx)
    me = lax.axis_index("ctx")
    i0, i1 = me // n1, me % n1
    span = rows // 2
    half_keys = n_ctx * span
    q_rows = GROUP * rows
    skip = q_rows // 2 // 128 * 128
    scale = 1.0 / math.sqrt(HEAD_DIM)
    to_exp2 = scale * math.log2(math.e)

    class Kind:
        def __init__(self, index):
            self.index = index
            first_is_0 = kinds[index] == 0
            self.nf, self.ns = (n0, n1) if first_is_0 else (n1, n0)
            self.f, self.s = (i0, i1) if first_is_0 else (i1, i0)
            self.first_is_0 = first_is_0

        def device(self, f, s):
            return f * n1 + s if self.first_is_0 else s * n1 + f

        def slot(self, f, s):
            return s * self.nf + f

        def neighbour(self, line, direction):
            step = 1 if direction == UP else -1
            if line == 0:
                return self.device(self.f + step, self.s)
            return self.device(self.f, self.s + step)

        def has(self, line, direction):
            x, n = (self.f, self.nf) if line == 0 else (self.s, self.ns)
            return x + 1 < n if direction == UP else x > 0

    kind_list = [Kind(i) for i in range(len(kinds))]

    def kind_of(h):
        return kind_list[h % len(kinds)]

    def block(slot):
        return pl.ds(pl.multiple_of(slot * span, span), span)

    first_span, second_span = order_ref[2 * me], order_ref[2 * me + 1]
    low_first = first_span < second_span

    def sort_halves(a, b):
        return jnp.where(low_first, a, b), jnp.where(low_first, b, a)

    barrier = pltpu.get_barrier_semaphore()
    base = kind_list[0]
    for line in (0, 1):
        for direction in (UP, DOWN):
            @pl.when(base.has(line, direction))
            def _(line=line, direction=direction):
                pl.semaphore_signal(
                    barrier, inc=1, device_id={"ctx": base.neighbour(line, direction)},
                    device_id_type=MESH,
                )
    peers = sum(
        base.has(line, direction).astype(jnp.int32) for line in (0, 1) for direction in (UP, DOWN)
    )
    pl.semaphore_wait(barrier, peers)

    def ag_copy(h, slot, line, direction):
        kind = kind_of(h)
        return pltpu.make_async_remote_copy(
            src_ref=kv.at[h, :, block(slot)],
            dst_ref=kv.at[h, :, block(slot)],
            send_sem=ag_send.at[h, slot, 2 * line + direction],
            recv_sem=ag_recv.at[h, slot],
            device_id={"ctx": kind.neighbour(line, direction)},
            device_id_type=MESH,
        )

    def ag_stage(h, stage, op):
        kind = kind_of(h)
        nf, ns, f, s = kind.nf, kind.ns, kind.f, kind.s

        def push(slot, line, direction):
            @pl.when(kind.has(line, direction))
            def _():
                copy = ag_copy(h, slot, line, direction)
                if op == "go":
                    copy.start()
                else:
                    copy.wait_send()

        def arrived(slot):
            if op == "go":
                ag_copy(h, slot, 0, UP).wait_recv()

        if stage == 0:
            own = kind.slot(f, s)
            if op == "go":
                columns = pl.ds(h * HEAD_DIM, HEAD_DIM)
                for ref, lanes in ((k_ref, pl.ds(0, HEAD_DIM)), (v_ref, pl.ds(HEAD_DIM, HEAD_DIM))):
                    low, high = sort_halves(ref[0:span, columns], ref[span:, columns])
                    kv[h, 0, block(own), lanes] = low
                    kv[h, 1, block(own), lanes] = high
            for line in (0, 1):
                push(own, line, UP)
                push(own, line, DOWN)
        elif stage < nf:
            for origin, direction in ((f - stage, UP), (f + stage, DOWN)):
                @pl.when(jnp.logical_and(origin >= 0, origin < nf))
                def _(origin=origin, direction=direction):
                    slot = kind.slot(origin, s)
                    arrived(slot)
                    push(slot, 0, direction)
                    push(slot, 1, UP)
                    push(slot, 1, DOWN)
        else:
            d = stage - nf + 1
            for origin, direction in ((s - d, UP), (s + d, DOWN)):
                @pl.when(jnp.logical_and(origin >= 0, origin < ns))
                def _(origin=origin, direction=direction):
                    for from_f in range(nf):
                        slot = kind.slot(from_f, origin)
                        arrived(slot)
                        push(slot, 1, direction)

    def ag_stages(h):
        return kind_of(h).nf + kind_of(h).ns - 1

    def s_copy(h, slot, direction):
        kind = kind_of(h)
        return pltpu.make_async_remote_copy(
            src_ref=send_s.at[h, :, block(slot)],
            dst_ref=recv_s.at[h, direction, :, block(slot)],
            send_sem=s_send.at[h, slot],
            recv_sem=s_recv.at[h, direction, slot],
            device_id={"ctx": kind.device(kind.f, kind.s + 1 - 2 * direction)},
            device_id_type=MESH,
        )

    def f_copy(h, x, direction):
        kind = kind_of(h)
        return pltpu.make_async_remote_copy(
            src_ref=send_f.at[h, :, block(x)],
            dst_ref=recv_f.at[h, direction, :, block(x)],
            send_sem=f_send.at[h, x],
            recv_sem=f_recv.at[h, direction, x],
            device_id={"ctx": kind.neighbour(0, direction)},
            device_id_type=MESH,
        )

    def s_pass_on(h, slot, direction, first):
        total = acc[h, :, block(slot)]
        copy = s_copy(h, slot, direction)
        if not first:
            copy.wait_recv()
            total = total + recv_s[h, direction, :, block(slot)].astype(jnp.float32)
        send_s[h, :, block(slot)] = total.astype(jnp.bfloat16)
        copy.start()

    def s_stage(h, stage):
        kind = kind_of(h)
        n = kind.ns

        @pl.when(kind.s == stage)
        def _():
            for x in range(n - 1, stage, -1):
                for f in range(kind.nf):
                    s_pass_on(h, kind.slot(f, x), UP, False)

        @pl.when(kind.s == n - 1 - stage)
        def _():
            for x in range(0, n - 1 - stage):
                for f in range(kind.nf):
                    s_pass_on(h, kind.slot(f, x), DOWN, False)

    def take_s(h, slot):
        kind = kind_of(h)
        for direction, there in ((UP, kind.s > 0), (DOWN, kind.s < kind.ns - 1)):
            @pl.when(there)
            def _(direction=direction):
                s_copy(h, slot, direction).wait_recv()
                where = block(slot)
                acc[h, :, where] = acc[h, :, where] + recv_s[h, direction, :, where].astype(jnp.float32)

    def f_stage(h, stage):
        kind = kind_of(h)
        n = kind.nf

        def pass_on(x, direction):
            slot = kind.slot(x, kind.s)
            take_s(h, slot)
            total = acc[h, :, block(slot)]
            copy = f_copy(h, x, direction)
            if stage > 0:
                copy.wait_recv()
                total = total + recv_f[h, direction, :, block(x)].astype(jnp.float32)
            send_f[h, :, block(x)] = total.astype(jnp.bfloat16)
            copy.start()

        @pl.when(kind.f == stage)
        def _():
            for x in range(n - 1, stage, -1):
                pass_on(x, UP)

        @pl.when(kind.f == n - 1 - stage)
        def _():
            for x in range(0, n - 1 - stage):
                pass_on(x, DOWN)

    def finish(h):
        kind = kind_of(h)
        own = kind.slot(kind.f, kind.s)
        take_s(h, own)
        where = block(own)
        for direction, there in ((UP, kind.f > 0), (DOWN, kind.f < kind.nf - 1)):
            @pl.when(there)
            def _(direction=direction):
                f_copy(h, kind.f, direction).wait_recv()
                acc[h, :, where] = acc[h, :, where] + recv_f[
                    h, direction, :, block(kind.f)
                ].astype(jnp.float32)
        columns = pl.ds(h * HEAD_DIM, HEAD_DIM)
        both = sort_halves(acc[h, 0, where], acc[h, 1, where])
        for i in range(2):
            rows_here = pl.ds(i * span, span)
            dk_ref[rows_here, columns] = (both[i][:, :HEAD_DIM] * scale).astype(jnp.bfloat16)
            dv_ref[rows_here, columns] = both[i][:, HEAD_DIM:].astype(jnp.bfloat16)

    def rs_tasks(h):
        kind = kind_of(h)
        tasks = [functools.partial(s_stage, h, stage) for stage in range(1, kind.ns - 1)]
        tasks += [functools.partial(f_stage, h, stage) for stage in range(kind.nf - 1)]
        return tasks + [functools.partial(finish, h)]

    def make_bias(kind):
        lane = lax.broadcasted_iota(jnp.int32, (1, q_rows), 1)
        low = jnp.minimum(first_span, second_span) * span
        high = jnp.maximum(first_span, second_span) * span
        q_pos = lane % span + jnp.where(lane < GROUP * span, low, high)
        row = lax.broadcasted_iota(jnp.int32, (span, q_rows), 0)

        @pl.loop(0, n_ctx)
        def _(slot):
            source = kind.device(slot % kind.nf, slot // kind.nf)
            a, b = order_ref[2 * source], order_ref[2 * source + 1]
            for half, start in ((0, jnp.minimum(a, b)), (1, jnp.maximum(a, b))):
                visible = row + start * span <= q_pos
                bias[kind.index, half, block(slot)] = jnp.where(visible, 0.0, NEG)

    halves = ((0, 0), (1, skip))

    def load_queries(h):
        for g in range(GROUP):
            columns = pl.ds((h * GROUP + g) * HEAD_DIM, HEAD_DIM)
            for ref, to in ((q_ref, qs), (g_ref, gs)):
                low, high = sort_halves(ref[0:span, columns], ref[span:, columns])
                to[pl.ds(g * span, span)] = low
                to[pl.ds((GROUP + g) * span, span)] = high

    def write_rows(ref, h, result):
        for g in range(GROUP):
            columns = pl.ds((h * GROUP + g) * HEAD_DIM, HEAD_DIM)
            first, second = sort_halves(
                result[g * span:(g + 1) * span],
                result[(GROUP + g) * span:(GROUP + g + 1) * span],
            )
            ref[0:span, columns] = first
            ref[span:, columns] = second

    def rows_of(i, size):
        return pl.ds(pl.multiple_of(i * size, size), size)

    tall = min(half_keys, 8 * span)

    def fold(x, op):
        return op(x.reshape(x.shape[0] // 8, 8, x.shape[1]), axis=0)

    def join(parts, op):
        low, high = (op(x, axis=0, keepdims=True) for x in parts)
        both = op(jnp.concatenate([low[:, skip:], high], axis=0), axis=0, keepdims=True)
        return jnp.concatenate([low[:, :skip], both], axis=1)

    def scores_pass(h):
        kind = kind_of(h)

        def body(i, tops):
            where = rows_of(i, tall)
            out = []
            for half, lanes in halves:
                s = dot_nt(kv[h, half, where, 0:HEAD_DIM], qs[lanes:])
                s = s + bias[kind.index, half, where, lanes:]
                probs[half, where, lanes:] = s
                out.append(jnp.maximum(tops[half], fold(s, jnp.max)))
            return tuple(out)

        tops = lax.fori_loop(
            0, half_keys // tall, body,
            tuple(jnp.full((8, q_rows - lanes), NEG, jnp.float32) for _, lanes in halves),
        )
        return join(tops, jnp.max) * to_exp2

    def weights_pass(h, top):
        att_t[...] = jnp.zeros_like(att_t)

        def body(i, totals):
            where = rows_of(i, tall)
            out = []
            for half, lanes in halves:
                e = jnp.exp2(probs[half, where, lanes:] * to_exp2 - top[:, lanes:])
                probs[half, where, lanes:] = e
                att_t[:, lanes:] += dot_tn(kv[h, half, where, HEAD_DIM:], e.astype(jnp.bfloat16))
                out.append(totals[half] + fold(e, jnp.sum))
            return tuple(out)

        totals = lax.fori_loop(
            0, half_keys // tall, body,
            tuple(jnp.zeros((8, q_rows - lanes), jnp.float32) for _, lanes in halves),
        )
        inverse = 1.0 / join(totals, jnp.sum)
        attention = (att_t[...] * inverse).T.astype(jnp.bfloat16)
        write_rows(att_ref, h, attention)
        product = gs[...].astype(jnp.float32) * attention.astype(jnp.float32)
        row_dot = jnp.sum(product.T, axis=0, keepdims=True)
        return inverse, row_dot

    def backward_group(h, s, inverse, row_dot, send):
        kind = kind_of(h)
        where = rows_of(s, kind.nf * span)
        low_grads = []
        for half, lanes in halves:
            v = kv[h, half, where, HEAD_DIM:]
            p = probs[half, where, lanes:] * inverse[:, lanes:]
            ds = (p * (dot_nt(v, gs[lanes:]) - row_dot[:, lanes:])).astype(jnp.bfloat16)
            acc[h, half, where, 0:HEAD_DIM] = dot_nn(ds, qs[lanes:])
            acc[h, half, where, HEAD_DIM:] = dot_nn(p.astype(jnp.bfloat16), gs[lanes:])
            low_grads.append(ds)
        if send:
            direction = jnp.where(s > kind.s, UP, DOWN)
            first = jnp.logical_or(
                jnp.logical_and(s > kind.s, kind.s == 0),
                jnp.logical_and(s < kind.s, kind.s == kind.ns - 1),
            )
            backwards = kind.f < kind.nf // 2

            @pl.when(first)
            def _():
                for b in range(kind.nf):
                    b = jnp.where(backwards, kind.nf - 1 - b, b)
                    s_pass_on(h, s * kind.nf + b, direction, True)

        for (half, lanes), ds in zip(halves, low_grads):
            dq_t[:, lanes:] += dot_tn(kv[h, half, where, 0:HEAD_DIM], ds)

    def write_dq(h):
        write_rows(dq_ref, h, (dq_t[...] * scale).T.astype(jnp.bfloat16))

    lag = 1
    ticks = []
    last_tick = lag * (kv_heads - 1) + max(ag_stages(h) for h in range(kv_heads))
    for t in range(last_tick):
        ticks.append([
            (h, t - lag * h) for h in range(kv_heads) if 0 <= t - lag * h < ag_stages(h)
        ])
    done = 0

    def run_ticks(until):
        nonlocal done
        while done < min(until, len(ticks)):
            for h, stage in ticks[done]:
                ag_stage(h, stage, "go")
            done += 1

    chains = []

    def advance():
        for chain in list(chains):
            chain.pop(0)()
            if not chain:
                chains.remove(chain)

    run_ticks(1)
    for kind in kind_list:
        make_bias(kind)
    load_queries(0)
    for h in range(kv_heads):
        kind = kind_of(h)
        run_ticks(lag * h + ag_stages(h))
        if h:
            load_queries(h)
        top = scores_pass(h)
        run_ticks(done + 1)
        inverse, row_dot = weights_pass(h, top)
        run_ticks(done + 1)
        advance()
        dq_t[...] = jnp.zeros_like(dq_t)

        def away(j, _):
            backward_group(h, lax.rem(kind.s + j, kind.ns), inverse, row_dot, True)
            return 0

        lax.fori_loop(1, kind.ns, away, 0)
        run_ticks(done + 1)
        backward_group(h, kind.s, inverse, row_dot, False)
        advance()
        chains.append(rs_tasks(h))
        if h == kv_heads - 1:
            advance()
        write_dq(h)
    while chains:
        advance()

    for h in range(kv_heads):
        kind = kind_of(h)
        for stage in range(ag_stages(h)):
            ag_stage(h, stage, "sent")

        def sent(j, _):
            group = lax.rem(kind.s + j, kind.ns)
            for f in range(kind.nf):
                s_copy(h, kind.slot(f, group), UP).wait_send()
            return 0

        lax.fori_loop(1, kind.ns, sent, 0)
        for j in range(1, kind.nf):
            f_copy(h, lax.rem(kind.f + j, kind.nf), UP).wait_send()


def copy_kernel(*refs):
    sems = refs[-1]
    count = (len(refs) - 1) // 2
    copies = [
        pltpu.make_async_copy(refs[i], refs[count + i], sems.at[i]) for i in range(count)
    ]
    for copy in copies:
        copy.start()
    for copy in copies:
        copy.wait()


def hand_out(results):
    anywhere = pl.BlockSpec(memory_space=pl.ANY)
    return pl.pallas_call(
        copy_kernel,
        out_shape=[jax.ShapeDtypeStruct(x.shape, x.dtype) for x in results],
        in_specs=[pl.BlockSpec(memory_space=pltpu.VMEM)] * len(results),
        out_specs=[anywhere] * len(results),
        scratch_shapes=[pltpu.SemaphoreType.DMA((len(results),))],
        name="hand_out",
    )(*results)


def on_device(n_ctx, queries, keys, values, out_grad, order):
    rows = queries.shape[0]
    kv_heads = keys.shape[1] // HEAD_DIM
    q_rows = GROUP * rows
    half_keys = n_ctx * rows // 2
    n0, n1 = line_lengths(n_ctx)
    kinds = (0,)
    wide = 2 * HEAD_DIM
    longest = max(n0, n1)
    vmem = pl.BlockSpec(memory_space=pltpu.VMEM)
    results = pl.pallas_call(
        functools.partial(kernel, n_ctx, kv_heads, rows, kinds),
        out_shape=[
            jax.ShapeDtypeStruct(x.shape, jnp.bfloat16) for x in (queries, queries, keys, values)
        ],
        in_specs=[vmem] * 4 + [pl.BlockSpec(memory_space=pltpu.SMEM)],
        out_specs=[vmem] * 4,
        scratch_shapes=[
            pltpu.VMEM((kv_heads, 2, half_keys, wide), jnp.bfloat16),
            pltpu.VMEM((len(kinds), 2, half_keys, q_rows), jnp.float32),
            pltpu.VMEM((2, half_keys, q_rows), jnp.float32),
            pltpu.VMEM((q_rows, HEAD_DIM), jnp.bfloat16),
            pltpu.VMEM((q_rows, HEAD_DIM), jnp.bfloat16),
            pltpu.VMEM((HEAD_DIM, q_rows), jnp.float32),
            pltpu.VMEM((HEAD_DIM, q_rows), jnp.float32),
            pltpu.VMEM((kv_heads, 2, half_keys, wide), jnp.float32),
            pltpu.VMEM((kv_heads, 2, half_keys, wide), jnp.bfloat16),
            pltpu.VMEM((kv_heads, 2, 2, half_keys, wide), jnp.bfloat16),
            pltpu.VMEM((kv_heads, 2, longest * rows // 2, wide), jnp.bfloat16),
            pltpu.VMEM((kv_heads, 2, 2, longest * rows // 2, wide), jnp.bfloat16),
            pltpu.SemaphoreType.DMA((kv_heads, n_ctx, 4)),
            pltpu.SemaphoreType.DMA((kv_heads, n_ctx)),
            pltpu.SemaphoreType.DMA((kv_heads, n_ctx)),
            pltpu.SemaphoreType.DMA((kv_heads, 2, n_ctx)),
            pltpu.SemaphoreType.DMA((kv_heads, longest)),
            pltpu.SemaphoreType.DMA((kv_heads, 2, longest)),
        ],
        compiler_params=pltpu.CompilerParams(
            collective_id=0, has_side_effects=True, vmem_limit_bytes=60 * 1024 * 1024
        ),
        name="attention_fwd_bwd",
    )(queries, keys, values, out_grad, order)
    return tuple(hand_out(results))


def solution(mesh):
    return jax.shard_map(
        functools.partial(on_device, mesh.shape["ctx"]),
        mesh=mesh,
        in_specs=(P("ctx", "head"), P("ctx", "head"), P("ctx", "head"), P("ctx", "head"), P()),
        out_specs=(P("ctx", "head"), P("ctx", "head"), P("ctx", "head"), P("ctx", "head")),
        check_vma=False,
    )
```

```python
import functools
import math

import jax
import jax.numpy as jnp
from jax import lax
from jax.experimental import pallas as pl
from jax.experimental.pallas import tpu as pltpu
from jax.sharding import PartitionSpec as P

HEADS = 32
KV_HEADS = 8
HEAD_DIM = 128
GROUP = HEADS // KV_HEADS
NEG = -1e30
MESH = pl.DeviceIdType.MESH

UP, DOWN = 0, 1


def line_lengths(n_ctx):
    n0 = 4 if n_ctx % 4 == 0 else 1
    return n0, n_ctx // n0


def dot_nt(a, b):
    return lax.dot_general(a, b, (((1,), (1,)), ((), ())), preferred_element_type=jnp.float32)


def dot_tn(a, b):
    return lax.dot_general(a, b, (((0,), (0,)), ((), ())), preferred_element_type=jnp.float32)


def dot_nn(a, b):
    return lax.dot_general(a, b, (((1,), (0,)), ((), ())), preferred_element_type=jnp.float32)


def kernel(
    n_ctx, kv_heads, rows, kinds,
    q_ref, k_ref, v_ref, g_ref, order_ref,
    att_ref, dq_ref, dk_ref, dv_ref,
    kv, bias, probs, qs, gs, att_t, dq_t, acc,
    send_s, recv_s, send_f, recv_f,
    ag_send, ag_recv, s_send, s_recv, f_send, f_recv,
):
    n0, n1 = line_lengths(n_ctx)
    me = lax.axis_index("ctx")
    i0, i1 = me // n1, me % n1
    span = rows // 2
    half_keys = n_ctx * span
    q_rows = GROUP * rows
    skip = q_rows // 2 // 128 * 128
    scale = 1.0 / math.sqrt(HEAD_DIM)
    to_exp2 = scale * math.log2(math.e)

    class Kind:
        def __init__(self, index):
            self.index = index
            first_is_0 = kinds[index] == 0
            self.nf, self.ns = (n0, n1) if first_is_0 else (n1, n0)
            self.f, self.s = (i0, i1) if first_is_0 else (i1, i0)
            self.first_is_0 = first_is_0

        def device(self, f, s):
            return f * n1 + s if self.first_is_0 else s * n1 + f

        def slot(self, f, s):
            return s * self.nf + f

        def neighbour(self, line, direction):
            step = 1 if direction == UP else -1
            if line == 0:
                return self.device(self.f + step, self.s)
            return self.device(self.f, self.s + step)

        def has(self, line, direction):
            x, n = (self.f, self.nf) if line == 0 else (self.s, self.ns)
            return x + 1 < n if direction == UP else x > 0

    kind_list = [Kind(i) for i in range(len(kinds))]

    def kind_of(h):
        return kind_list[h % len(kinds)]

    def block(slot):
        return pl.ds(pl.multiple_of(slot * span, span), span)

    first_span, second_span = order_ref[2 * me], order_ref[2 * me + 1]
    low_first = first_span < second_span

    def sort_halves(a, b):
        return jnp.where(low_first, a, b), jnp.where(low_first, b, a)

    barrier = pltpu.get_barrier_semaphore()
    base = kind_list[0]
    for line in (0, 1):
        for direction in (UP, DOWN):
            @pl.when(base.has(line, direction))
            def _(line=line, direction=direction):
                pl.semaphore_signal(
                    barrier, inc=1, device_id={"ctx": base.neighbour(line, direction)},
                    device_id_type=MESH,
                )
    peers = sum(
        base.has(line, direction).astype(jnp.int32) for line in (0, 1) for direction in (UP, DOWN)
    )
    pl.semaphore_wait(barrier, peers)

    def ag_copy(h, slot, line, direction):
        kind = kind_of(h)
        return pltpu.make_async_remote_copy(
            src_ref=kv.at[h, :, block(slot)],
            dst_ref=kv.at[h, :, block(slot)],
            send_sem=ag_send.at[h, slot, 2 * line + direction],
            recv_sem=ag_recv.at[h, slot],
            device_id={"ctx": kind.neighbour(line, direction)},
            device_id_type=MESH,
        )

    def ag_stage(h, stage, op):
        kind = kind_of(h)
        nf, ns, f, s = kind.nf, kind.ns, kind.f, kind.s

        def push(slot, line, direction):
            @pl.when(kind.has(line, direction))
            def _():
                copy = ag_copy(h, slot, line, direction)
                if op == "go":
                    copy.start()
                else:
                    copy.wait_send()

        def arrived(slot):
            if op == "go":
                ag_copy(h, slot, 0, UP).wait_recv()

        if stage == 0:
            own = kind.slot(f, s)
            if op == "go":
                columns = pl.ds(h * HEAD_DIM, HEAD_DIM)
                for ref, lanes in ((k_ref, pl.ds(0, HEAD_DIM)), (v_ref, pl.ds(HEAD_DIM, HEAD_DIM))):
                    low, high = sort_halves(ref[0:span, columns], ref[span:, columns])
                    kv[h, 0, block(own), lanes] = low
                    kv[h, 1, block(own), lanes] = high
            for line in (0, 1):
                push(own, line, UP)
                push(own, line, DOWN)
        elif stage < nf:
            for origin, direction in ((f - stage, UP), (f + stage, DOWN)):
                @pl.when(jnp.logical_and(origin >= 0, origin < nf))
                def _(origin=origin, direction=direction):
                    slot = kind.slot(origin, s)
                    arrived(slot)
                    push(slot, 0, direction)
                    push(slot, 1, UP)
                    push(slot, 1, DOWN)
        else:
            d = stage - nf + 1
            for origin, direction in ((s - d, UP), (s + d, DOWN)):
                @pl.when(jnp.logical_and(origin >= 0, origin < ns))
                def _(origin=origin, direction=direction):
                    for from_f in range(nf):
                        slot = kind.slot(from_f, origin)
                        arrived(slot)
                        push(slot, 1, direction)

    def ag_stages(h):
        return kind_of(h).nf + kind_of(h).ns - 1

    def s_copy(h, slot, direction):
        kind = kind_of(h)
        return pltpu.make_async_remote_copy(
            src_ref=send_s.at[h, :, block(slot)],
            dst_ref=recv_s.at[h, direction, :, block(slot)],
            send_sem=s_send.at[h, slot],
            recv_sem=s_recv.at[h, direction, slot],
            device_id={"ctx": kind.device(kind.f, kind.s + 1 - 2 * direction)},
            device_id_type=MESH,
        )

    def f_copy(h, x, direction):
        kind = kind_of(h)
        return pltpu.make_async_remote_copy(
            src_ref=send_f.at[h, :, block(x)],
            dst_ref=recv_f.at[h, direction, :, block(x)],
            send_sem=f_send.at[h, x],
            recv_sem=f_recv.at[h, direction, x],
            device_id={"ctx": kind.neighbour(0, direction)},
            device_id_type=MESH,
        )

    def s_pass_on(h, slot, direction, first):
        total = acc[h, :, block(slot)]
        copy = s_copy(h, slot, direction)
        if not first:
            copy.wait_recv()
            total = total + recv_s[h, direction, :, block(slot)].astype(jnp.float32)
        send_s[h, :, block(slot)] = total.astype(jnp.bfloat16)
        copy.start()

    def s_stage(h, stage):
        kind = kind_of(h)
        n = kind.ns

        @pl.when(kind.s == stage)
        def _():
            for x in range(n - 1, stage, -1):
                for f in range(kind.nf):
                    s_pass_on(h, kind.slot(f, x), UP, False)

        @pl.when(kind.s == n - 1 - stage)
        def _():
            for x in range(0, n - 1 - stage):
                for f in range(kind.nf):
                    s_pass_on(h, kind.slot(f, x), DOWN, False)

    def take_s(h, slot):
        kind = kind_of(h)
        for direction, there in ((UP, kind.s > 0), (DOWN, kind.s < kind.ns - 1)):
            @pl.when(there)
            def _(direction=direction):
                s_copy(h, slot, direction).wait_recv()
                where = block(slot)
                acc[h, :, where] = acc[h, :, where] + recv_s[h, direction, :, where].astype(jnp.float32)

    def f_stage(h, stage):
        kind = kind_of(h)
        n = kind.nf

        def pass_on(x, direction):
            slot = kind.slot(x, kind.s)
            take_s(h, slot)
            total = acc[h, :, block(slot)]
            copy = f_copy(h, x, direction)
            if stage > 0:
                copy.wait_recv()
                total = total + recv_f[h, direction, :, block(x)].astype(jnp.float32)
            send_f[h, :, block(x)] = total.astype(jnp.bfloat16)
            copy.start()

        @pl.when(kind.f == stage)
        def _():
            for x in range(n - 1, stage, -1):
                pass_on(x, UP)

        @pl.when(kind.f == n - 1 - stage)
        def _():
            for x in range(0, n - 1 - stage):
                pass_on(x, DOWN)

    def finish(h):
        kind = kind_of(h)
        own = kind.slot(kind.f, kind.s)
        take_s(h, own)
        where = block(own)
        for direction, there in ((UP, kind.f > 0), (DOWN, kind.f < kind.nf - 1)):
            @pl.when(there)
            def _(direction=direction):
                f_copy(h, kind.f, direction).wait_recv()
                acc[h, :, where] = acc[h, :, where] + recv_f[
                    h, direction, :, block(kind.f)
                ].astype(jnp.float32)
        columns = pl.ds(h * HEAD_DIM, HEAD_DIM)
        both = sort_halves(acc[h, 0, where], acc[h, 1, where])
        for i in range(2):
            rows_here = pl.ds(i * span, span)
            dk_ref[rows_here, columns] = (both[i][:, :HEAD_DIM] * scale).astype(jnp.bfloat16)
            dv_ref[rows_here, columns] = both[i][:, HEAD_DIM:].astype(jnp.bfloat16)

    def rs_tasks(h):
        kind = kind_of(h)
        tasks = [functools.partial(s_stage, h, stage) for stage in range(1, kind.ns - 1)]
        tasks += [functools.partial(f_stage, h, stage) for stage in range(kind.nf - 1)]
        return tasks + [functools.partial(finish, h)]

    def make_bias(kind):
        lane = lax.broadcasted_iota(jnp.int32, (1, q_rows), 1)
        low = jnp.minimum(first_span, second_span) * span
        high = jnp.maximum(first_span, second_span) * span
        q_pos = lane % span + jnp.where(lane < GROUP * span, low, high)
        row = lax.broadcasted_iota(jnp.int32, (span, q_rows), 0)

        @pl.loop(0, n_ctx)
        def _(slot):
            source = kind.device(slot % kind.nf, slot // kind.nf)
            a, b = order_ref[2 * source], order_ref[2 * source + 1]
            for half, start in ((0, jnp.minimum(a, b)), (1, jnp.maximum(a, b))):
                visible = row + start * span <= q_pos
                bias[kind.index, half, block(slot)] = jnp.where(visible, 0.0, NEG)

    halves = ((0, 0), (1, skip))

    def load_queries(h):
        for g in range(GROUP):
            columns = pl.ds((h * GROUP + g) * HEAD_DIM, HEAD_DIM)
            for ref, to in ((q_ref, qs), (g_ref, gs)):
                low, high = sort_halves(ref[0:span, columns], ref[span:, columns])
                to[pl.ds(g * span, span)] = low
                to[pl.ds((GROUP + g) * span, span)] = high

    def write_rows(ref, h, result):
        for g in range(GROUP):
            columns = pl.ds((h * GROUP + g) * HEAD_DIM, HEAD_DIM)
            first, second = sort_halves(
                result[g * span:(g + 1) * span],
                result[(GROUP + g) * span:(GROUP + g + 1) * span],
            )
            ref[0:span, columns] = first
            ref[span:, columns] = second

    def rows_of(i, size):
        return pl.ds(pl.multiple_of(i * size, size), size)

    tall = min(half_keys, 8 * span)

    def fold(x, op):
        return op(x.reshape(x.shape[0] // 8, 8, x.shape[1]), axis=0)

    def join(parts, op):
        low, high = (op(x, axis=0, keepdims=True) for x in parts)
        both = op(jnp.concatenate([low[:, skip:], high], axis=0), axis=0, keepdims=True)
        return jnp.concatenate([low[:, :skip], both], axis=1)

    def scores_pass(h):
        kind = kind_of(h)

        def body(i, tops):
            where = rows_of(i, tall)
            out = []
            for half, lanes in halves:
                s = dot_nt(kv[h, half, where, 0:HEAD_DIM], qs[lanes:])
                s = s + bias[kind.index, half, where, lanes:]
                probs[half, where, lanes:] = s
                out.append(jnp.maximum(tops[half], fold(s, jnp.max)))
            return tuple(out)

        tops = lax.fori_loop(
            0, half_keys // tall, body,
            tuple(jnp.full((8, q_rows - lanes), NEG, jnp.float32) for _, lanes in halves),
        )
        return join(tops, jnp.max) * to_exp2

    def weights_pass(h, top):
        att_t[...] = jnp.zeros_like(att_t)

        def body(i, totals):
            where = rows_of(i, tall)
            out = []
            for half, lanes in halves:
                e = jnp.exp2(probs[half, where, lanes:] * to_exp2 - top[:, lanes:])
                probs[half, where, lanes:] = e
                att_t[:, lanes:] += dot_tn(kv[h, half, where, HEAD_DIM:], e.astype(jnp.bfloat16))
                out.append(totals[half] + fold(e, jnp.sum))
            return tuple(out)

        totals = lax.fori_loop(
            0, half_keys // tall, body,
            tuple(jnp.zeros((8, q_rows - lanes), jnp.float32) for _, lanes in halves),
        )
        inverse = 1.0 / join(totals, jnp.sum)
        attention = (att_t[...] * inverse).T.astype(jnp.bfloat16)
        write_rows(att_ref, h, attention)
        product = gs[...].astype(jnp.float32) * attention.astype(jnp.float32)
        row_dot = jnp.sum(product.T, axis=0, keepdims=True)
        return inverse, row_dot

    def backward_group(h, s, inverse, row_dot, send):
        kind = kind_of(h)
        where = rows_of(s, kind.nf * span)
        low_grads = []
        for half, lanes in halves:
            v = kv[h, half, where, HEAD_DIM:]
            p = probs[half, where, lanes:] * inverse[:, lanes:]
            ds = (p * (dot_nt(v, gs[lanes:]) - row_dot[:, lanes:])).astype(jnp.bfloat16)
            acc[h, half, where, 0:HEAD_DIM] = dot_nn(ds, qs[lanes:])
            acc[h, half, where, HEAD_DIM:] = dot_nn(p.astype(jnp.bfloat16), gs[lanes:])
            low_grads.append(ds)
        if send:
            direction = jnp.where(s > kind.s, UP, DOWN)
            first = jnp.logical_or(
                jnp.logical_and(s > kind.s, kind.s == 0),
                jnp.logical_and(s < kind.s, kind.s == kind.ns - 1),
            )
            backwards = kind.f < kind.nf // 2

            @pl.when(first)
            def _():
                for b in range(kind.nf):
                    b = jnp.where(backwards, kind.nf - 1 - b, b)
                    s_pass_on(h, s * kind.nf + b, direction, True)

        for (half, lanes), ds in zip(halves, low_grads):
            dq_t[:, lanes:] += dot_tn(kv[h, half, where, 0:HEAD_DIM], ds)

    def write_dq(h):
        write_rows(dq_ref, h, (dq_t[...] * scale).T.astype(jnp.bfloat16))

    lag = 2
    ticks = []
    last_tick = lag * (kv_heads - 1) + max(ag_stages(h) for h in range(kv_heads))
    for t in range(last_tick):
        ticks.append([
            (h, t - lag * h) for h in range(kv_heads) if 0 <= t - lag * h < ag_stages(h)
        ])
    done = 0

    def run_ticks(until):
        nonlocal done
        while done < min(until, len(ticks)):
            for h, stage in ticks[done]:
                ag_stage(h, stage, "go")
            done += 1

    chains = []

    def advance():
        for chain in list(chains):
            chain.pop(0)()
            if not chain:
                chains.remove(chain)

    run_ticks(1)
    for kind in kind_list:
        make_bias(kind)
    load_queries(0)
    for h in range(kv_heads):
        kind = kind_of(h)
        run_ticks(lag * h + ag_stages(h))
        if h:
            load_queries(h)
        top = scores_pass(h)
        run_ticks(done + 1)
        inverse, row_dot = weights_pass(h, top)
        run_ticks(done + 1)
        advance()
        dq_t[...] = jnp.zeros_like(dq_t)

        def away(j, _):
            backward_group(h, lax.rem(kind.s + j, kind.ns), inverse, row_dot, True)
            return 0

        lax.fori_loop(1, kind.ns, away, 0)
        run_ticks(done + 1)
        backward_group(h, kind.s, inverse, row_dot, False)
        advance()
        chains.append(rs_tasks(h))
        if h == kv_heads - 1:
            advance()
        write_dq(h)
    while chains:
        advance()

    for h in range(kv_heads):
        kind = kind_of(h)
        for stage in range(ag_stages(h)):
            ag_stage(h, stage, "sent")

        def sent(j, _):
            group = lax.rem(kind.s + j, kind.ns)
            for f in range(kind.nf):
                s_copy(h, kind.slot(f, group), UP).wait_send()
            return 0

        lax.fori_loop(1, kind.ns, sent, 0)
        for j in range(1, kind.nf):
            f_copy(h, lax.rem(kind.f + j, kind.nf), UP).wait_send()


def copy_kernel(*refs):
    sems = refs[-1]
    count = (len(refs) - 1) // 2
    copies = [
        pltpu.make_async_copy(refs[i], refs[count + i], sems.at[i]) for i in range(count)
    ]
    for copy in copies:
        copy.start()
    for copy in copies:
        copy.wait()


def hand_out(results):
    anywhere = pl.BlockSpec(memory_space=pl.ANY)
    return pl.pallas_call(
        copy_kernel,
        out_shape=[jax.ShapeDtypeStruct(x.shape, x.dtype) for x in results],
        in_specs=[pl.BlockSpec(memory_space=pltpu.VMEM)] * len(results),
        out_specs=[anywhere] * len(results),
        scratch_shapes=[pltpu.SemaphoreType.DMA((len(results),))],
        name="hand_out",
    )(*results)


def on_device(n_ctx, queries, keys, values, out_grad, order):
    rows = queries.shape[0]
    kv_heads = keys.shape[1] // HEAD_DIM
    q_rows = GROUP * rows
    half_keys = n_ctx * rows // 2
    n0, n1 = line_lengths(n_ctx)
    kinds = (0,)
    wide = 2 * HEAD_DIM
    longest = max(n0, n1)
    vmem = pl.BlockSpec(memory_space=pltpu.VMEM)
    results = pl.pallas_call(
        functools.partial(kernel, n_ctx, kv_heads, rows, kinds),
        out_shape=[
            jax.ShapeDtypeStruct(x.shape, jnp.bfloat16) for x in (queries, queries, keys, values)
        ],
        in_specs=[vmem] * 4 + [pl.BlockSpec(memory_space=pltpu.SMEM)],
        out_specs=[vmem] * 4,
        scratch_shapes=[
            pltpu.VMEM((kv_heads, 2, half_keys, wide), jnp.bfloat16),
            pltpu.VMEM((len(kinds), 2, half_keys, q_rows), jnp.float32),
            pltpu.VMEM((2, half_keys, q_rows), jnp.float32),
            pltpu.VMEM((q_rows, HEAD_DIM), jnp.bfloat16),
            pltpu.VMEM((q_rows, HEAD_DIM), jnp.bfloat16),
            pltpu.VMEM((HEAD_DIM, q_rows), jnp.float32),
            pltpu.VMEM((HEAD_DIM, q_rows), jnp.float32),
            pltpu.VMEM((kv_heads, 2, half_keys, wide), jnp.float32),
            pltpu.VMEM((kv_heads, 2, half_keys, wide), jnp.bfloat16),
            pltpu.VMEM((kv_heads, 2, 2, half_keys, wide), jnp.bfloat16),
            pltpu.VMEM((kv_heads, 2, longest * rows // 2, wide), jnp.bfloat16),
            pltpu.VMEM((kv_heads, 2, 2, longest * rows // 2, wide), jnp.bfloat16),
            pltpu.SemaphoreType.DMA((kv_heads, n_ctx, 4)),
            pltpu.SemaphoreType.DMA((kv_heads, n_ctx)),
            pltpu.SemaphoreType.DMA((kv_heads, n_ctx)),
            pltpu.SemaphoreType.DMA((kv_heads, 2, n_ctx)),
            pltpu.SemaphoreType.DMA((kv_heads, longest)),
            pltpu.SemaphoreType.DMA((kv_heads, 2, longest)),
        ],
        compiler_params=pltpu.CompilerParams(
            collective_id=0, has_side_effects=True, vmem_limit_bytes=60 * 1024 * 1024
        ),
        name="attention_fwd_bwd",
    )(queries, keys, values, out_grad, order)
    return tuple(hand_out(results))


def solution(mesh):
    return jax.shard_map(
        functools.partial(on_device, mesh.shape["ctx"]),
        mesh=mesh,
        in_specs=(P("ctx", "head"), P("ctx", "head"), P("ctx", "head"), P("ctx", "head"), P()),
        out_specs=(P("ctx", "head"), P("ctx", "head"), P("ctx", "head"), P("ctx", "head")),
        check_vma=False,
    )
```
